32 devices in a mesh: group: 2 (over x), member: 16 (over z, y, core).
Axes of the slice: x: 2, y: 2, z: 4, core: 2. Of those that a mesh axis runs over, the one named last changes fastest.
Arguments:
- entities: bfloat16 [16384, 400], P(('group', 'member')), may hold values from -1.796875 to 1.796875
- hub_rows: bfloat16 [128, 400], replicated, may hold values from -1.796875 to 1.796875
- relations: float32 [2112, 400], replicated
- matching: int32 [2], replicated, may hold values from 0 to 1, as said below
- head_index: int32 [512, 256], P(('group', 'member')), may hold values from 0 to 511
- tail_index: int32 [512, 256], P(('group', 'member')), may hold values from 0 to 639
- tile_rel: int32 [512], P(('group', 'member')), may hold values from 0 to 2111
- tile_count: int32 [2, 16], P('group', 'member'), may hold values from 1 to 16, as said below
Outputs:
- new_entities: bfloat16 [16384, 400], P(('group', 'member'))
- new_hub: bfloat16 [128, 400], replicated
The draws below stay inside these ranges and needn't reach their ends.
Inputs may be any that keep to these rules, and one draw needn't show every extreme that they name: `matching`: a permutation of the partitions. `tile_count`: some device has exactly 16 live tiles.
All inputs are finite; a program needn't handle non-finite values.
Results may differ from the reference program's by a relative error of at most 0.014.
Values may be sent and summed in bfloat16 or wider, within the bound.
A program may use at most 64 MiB of HBM per device.

```python
import jax
import jax.numpy as jnp
from jax import lax

D = 400
RELS = 2112
HUB = 128
EDGE = 256
ROWS = 512
TILES = 16
GROUPS = 2
MEMBERS = 16
ENTITIES = 16384
ALLTILES = 512


def draw_relations(key, part):
    first = jax.random.fold_in(jax.random.fold_in(key, 11), 0)
    return jax.random.normal(first, (RELS, D), jnp.float32) * 1.2


def draw_matching(key, part):
    first, second = jax.random.split(jax.random.fold_in(key, 37))
    order = jax.random.permutation(first, GROUPS).astype(jnp.int32)
    if GROUPS <= 2:
        return order
    chosen = jax.random.randint(second, (), 0, GROUPS).astype(jnp.int32)
    target = (chosen + GROUPS // 2) % GROUPS
    places = jnp.arange(GROUPS, dtype=jnp.int32)
    holder = jnp.sum(jnp.where(order == target, places, 0)).astype(jnp.int32)
    old_value = jnp.sum(jnp.where(places == chosen, order, 0)).astype(jnp.int32)
    swapped = jnp.where(places == holder, old_value, order)
    swapped = jnp.where(places == chosen, target, swapped)
    return swapped.astype(jnp.int32)


def draw_tile_count(key, part):
    first, second = jax.random.split(jax.random.fold_in(key, 23))
    raw_draw = jax.random.randint(first, (GROUPS * MEMBERS,), 0, TILES)
    counts = 1 + raw_draw * raw_draw // TILES
    chosen = jax.random.randint(second, (), 0, GROUPS * MEMBERS)
    counts = jnp.where(jnp.arange(GROUPS * MEMBERS) == chosen, TILES, counts)
    return counts.reshape(GROUPS, MEMBERS).astype(jnp.int32)


def set_ends(entries, stream_key, low, largest):
    place = [jax.random.randint(jax.random.fold_in(stream_key, axis), (), 0, length) for axis, length in enumerate(entries.shape)]
    widest = entries.shape.index(max(entries.shape))
    beside = place[:widest] + [(place[widest] + 1) % entries.shape[widest]] + place[widest + 1:]
    return entries.at[tuple(place)].set(low).at[tuple(beside)].set(largest)


def block_scale(key, shape, shards, least, high):
    factor_of, own = 1.0, jax.random.fold_in(key, 6)
    for position, blocks in shards:
        steps = jnp.exp(jax.random.uniform(jax.random.fold_in(own, position), (blocks,), jnp.float32, least / len(shards), high / len(shards)))
        factor_of = factor_of * jnp.repeat(steps, shape[position] // blocks).reshape([-1 if axis == position else 1 for axis in range(len(shape))])
    return factor_of


def gaussian(key, shape, scale, bound, shards=(), kind=jnp.bfloat16):
    gain = block_scale(key, shape, shards, -0.22, 0.18) if shards else 1.0
    drawn = jax.random.normal(key, shape, jnp.float32) * scale * gain
    return jnp.minimum(jnp.maximum(drawn, -bound), bound).astype(kind)


def setup_inputs(seed: int = 0) -> dict:
    keys = jax.random.split(jax.random.key(seed), 9)
    return {
        "entities": gaussian(keys[0], (ENTITIES, D), 0.3, 1.796875, ((0, 32),)),
        "hub_rows": gaussian(keys[1], (HUB, D), 0.3, 1.796875),
        "relations": draw_relations(jax.random.fold_in(keys[8], 71), 0),
        "matching": draw_matching(jax.random.fold_in(keys[8], 71), 0),
        "head_index": set_ends(jax.random.randint(keys[4], (ALLTILES, EDGE), 0, ROWS), jax.random.fold_in(keys[4], 1), 0, ROWS - 1).astype(jnp.int32),
        "tail_index": set_ends(jax.random.randint(keys[5], (ALLTILES, EDGE), 0, ROWS + HUB), jax.random.fold_in(keys[5], 1), 0, (ROWS + HUB) - 1).astype(jnp.int32),
        "tile_rel": set_ends(jax.random.randint(keys[6], (ALLTILES,), 0, RELS), jax.random.fold_in(keys[6], 1), 0, RELS - 1).astype(jnp.int32),
        "tile_count": draw_tile_count(jax.random.fold_in(keys[8], 71), 0),
    }


learn_rate = 0.1


def rotate(rows, weight):
    half = rows.shape[1] // 2
    real_part = rows[:, :half]
    imag_part = rows[:, half:]
    w_real = weight[:half]
    w_imag = weight[half:]
    return jnp.concatenate([real_part * w_real - imag_part * w_imag, real_part * w_imag + imag_part * w_real], axis=1)


def pullback(grads, weight):
    half = grads.shape[1] // 2
    d_real = grads[:, :half]
    d_imag = grads[:, half:]
    w_real = weight[:half]
    w_imag = weight[half:]
    return jnp.concatenate([d_real * w_real + d_imag * w_imag, d_imag * w_real - d_real * w_imag], axis=1)


def tile_grads(head_pick, tail_pick, weight):
    query = rotate(head_pick.astype(jnp.float32), weight).astype(jnp.bfloat16)
    scores = jnp.dot(query, tail_pick.T, preferred_element_type=jnp.float32)
    top_score = jnp.max(scores, axis=1, keepdims=True)
    expo = jnp.exp(scores - top_score)
    probs = expo / jnp.sum(expo, axis=1, keepdims=True)
    diff = (probs - jnp.eye(scores.shape[0], dtype=jnp.float32)).astype(jnp.bfloat16)
    d_query = jnp.dot(diff, tail_pick, preferred_element_type=jnp.float32)
    d_tail = jnp.dot(diff.T, query, preferred_element_type=jnp.float32).astype(jnp.bfloat16)
    d_head = pullback(d_query, weight).astype(jnp.bfloat16)
    return d_head, d_tail


def reference(entities, hub_rows, relations, matching, head_index, tail_index, tile_rel, tile_count):
    blocks = entities.reshape(GROUPS, MEMBERS, ROWS, D)

    def device_grads(device):
        group_pos = device // MEMBERS
        member_pos = device % MEMBERS
        own_rows = blocks[group_pos, member_pos]
        partner = matching[group_pos]
        table = jnp.concatenate([blocks[partner, member_pos], hub_rows], axis=0)
        heads_dev = lax.dynamic_slice_in_dim(head_index, (device * TILES).astype(jnp.int32), TILES, 0)
        tails_dev = lax.dynamic_slice_in_dim(tail_index, (device * TILES).astype(jnp.int32), TILES, 0)
        rels_dev = lax.dynamic_slice_in_dim(tile_rel, (device * TILES).astype(jnp.int32), TILES, 0)
        tile_total = tile_count[group_pos, member_pos]

        def one_tile(tile_pos, grads):
            head_ids = heads_dev[tile_pos]
            tail_ids = tails_dev[tile_pos]
            weight = relations[rels_dev[tile_pos]]
            d_head, d_tail = tile_grads(own_rows[head_ids], table[tail_ids], weight)
            head_acc = grads[0] + jax.ops.segment_sum(d_head.astype(jnp.float32), head_ids, num_segments=ROWS)
            tail_acc = grads[1] + jax.ops.segment_sum(d_tail.astype(jnp.float32), tail_ids, num_segments=ROWS + HUB)
            return (head_acc, tail_acc)

        start_grads = (jnp.zeros((ROWS, D), jnp.float32), jnp.zeros((ROWS + HUB, D), jnp.float32))
        return lax.fori_loop(0, tile_total, one_tile, start_grads)

    head_grads, tail_grads = lax.map(device_grads, jnp.arange(GROUPS * MEMBERS, dtype=jnp.int32))
    back = tail_grads[:, :ROWS].astype(jnp.bfloat16).reshape(GROUPS, MEMBERS, ROWS, D)
    returned = jnp.zeros_like(back).at[matching].set(back)
    total = head_grads.reshape(GROUPS, MEMBERS, ROWS, D) + returned.astype(jnp.float32)
    new_entities = (blocks.astype(jnp.float32) - learn_rate * total).astype(jnp.bfloat16).reshape(ENTITIES, D)
    hub_grad = jnp.sum(tail_grads[:, ROWS:], axis=0)
    new_hub = (hub_rows.astype(jnp.float32) - learn_rate * hub_grad).astype(jnp.bfloat16)
    return (new_entities, new_hub)
```

```python
import functools

import jax
import jax.numpy as jnp
from jax import lax
from jax.experimental import pallas as pl
from jax.experimental.pallas import tpu as pltpu
from jax.sharding import PartitionSpec as P

learn_rate = 0.1
MESH = pl.DeviceIdType.MESH
LANES = 128
HALF = 256
WIDE = 2 * HALF
CHUNKS = 16
CHUNK_ROWS = 16
contract_first = (((0,), (0,)), ((), ()))
contract_last = (((1,), (1,)), ((), ()))
f32 = jnp.float32
bf16 = jnp.bfloat16


def widen(rows):
    half = rows.shape[1] // 2
    gap = jnp.zeros((rows.shape[0], HALF - half), rows.dtype)
    return jnp.concatenate([rows[:, :half], gap, rows[:, half:], gap], axis=1)


def narrow(rows, half):
    return jnp.concatenate([rows[:, :half], rows[:, HALF : HALF + half]], axis=1)


def fold(rest):
    rows, k = rest.shape
    parts = LANES // k
    step = rows // parts
    return jnp.concatenate([rest[i * step : (i + 1) * step] for i in range(parts)], axis=1)


def unfold(folded, k):
    return jnp.concatenate(
        [folded[:, i * k : (i + 1) * k] for i in range(LANES // k)], axis=0
    )


def kernel(
    groups, members, count_ref, rel_ref, match_ref,
    ent_ref, hub_ref, head_ref, tail_ref, table_ref,
    new_ent_ref, new_hub_ref,
    weights_all, ent_wide, tab_wide, hub_wide, peer_main, peer_rest, rest_send,
    head_col, tail_col, head_row, tail_row, weights, query, d_head, d_tail,
    back_main, back_rest, back_sum, hub_send, hub_in, hub_mid, hub_out,
    rel_sem, ent_send, ent_recv, back_send, back_recv,
    s1, r1, s2, r2, s3, r3,
):
    g = lax.axis_index("group")
    m = lax.axis_index("member")
    rows, width = ent_ref.shape
    half = width // 2
    hub_rows = hub_ref.shape[0]
    tiles, edge = head_ref.shape
    main = width // LANES * LANES
    rest = width - main
    parts = back_send.shape[0]
    part_rows = rows // parts
    part_rest = part_rows * rest // LANES

    load = pltpu.make_async_copy(table_ref, weights_all, rel_sem)
    load.start()
    other_groups = [lax.rem(g + d, groups) for d in range(1, groups)]
    other_members = [lax.rem(m + d, members) for d in range(1, members)]
    barrier = pltpu.get_barrier_semaphore()
    for o in other_groups:
        pl.semaphore_signal(barrier, inc=1, device_id=(o, m), device_id_type=MESH)
    for o in other_members:
        pl.semaphore_signal(barrier, inc=1, device_id=(g, o), device_id_type=MESH)

    rest_send[...] = fold(ent_ref[:, main:].astype(f32)).astype(bf16)
    pl.semaphore_wait(barrier, groups + members - 2)

    def remote(src, dst, send, recv, where):
        return pltpu.make_async_remote_copy(
            src_ref=src, dst_ref=dst, send_sem=send, recv_sem=recv,
            device_id=where, device_id_type=MESH,
        )

    sends = []
    for o in other_groups:
        sends.append(
            remote(ent_ref.at[:, pl.ds(0, main)], peer_main.at[g],
                   ent_send.at[0, o], ent_recv.at[0, g], (o, m)))
        sends.append(
            remote(rest_send, peer_rest.at[g], ent_send.at[1, o], ent_recv.at[1, g], (o, m)))
    for copy in sends:
        copy.start()

    own = ent_ref[...]
    peer_main[g] = own[:, :main]
    peer_rest[g] = rest_send[...]
    ent_wide[...] = widen(own.astype(f32)).astype(bf16)
    hub_w = widen(hub_ref[...].astype(f32))
    tab_wide[pl.ds(rows, hub_rows), :] = hub_w.astype(bf16)
    for c in range(CHUNKS):
        r, k = c // 2 * CHUNK_ROWS, c % 2 * HALF
        hub_wide[c] = hub_w[r : r + CHUNK_ROWS, k : k + HALF]
    heads, tails = head_ref[...], tail_ref[...]
    heads_t, tails_t = heads.T, tails.T
    for t in range(tiles):
        head_col[t] = heads_t[:, t : t + 1]
        tail_col[t] = tails_t[:, t : t + 1]
        head_row[:, t * edge : (t + 1) * edge] = heads[t : t + 1]
        tail_row[:, t * edge : (t + 1) * edge] = tails[t : t + 1]

    load.wait()
    live = count_ref[0, 0]
    picked = []
    for t in range(tiles):
        row = weights_all[pl.ds(rel_ref[t], 1), :]
        picked.append(jnp.where(t < live, row, jnp.zeros_like(row)))
    weights[...] = widen(jnp.concatenate(picked, axis=0))

    def hot(col, n):
        return (col == lax.broadcasted_iota(jnp.int32, (edge, n), 1)).astype(f32).astype(bf16)

    def make_query(t):
        head = jnp.dot(hot(head_col[t], rows), ent_wide[...], preferred_element_type=f32)
        w = weights[pl.ds(t, 1), :]
        wr, wi = w[:, :HALF], w[:, HALF:]
        hr, hi = head[:, :HALF], head[:, HALF:]
        query[t] = jnp.concatenate([hr * wr - hi * wi, hr * wi + hi * wr], axis=1).astype(bf16)

    def query_pair(i, _):
        make_query(2 * i)
        make_query(2 * i + 1)
        return 0

    lax.fori_loop(0, tiles // 2, query_pair, 0)

    for o in other_groups:
        remote(ent_ref.at[:, pl.ds(0, main)], peer_main.at[o],
               ent_send.at[0, o], ent_recv.at[0, o], (o, m)).wait_recv()
        remote(rest_send, peer_rest.at[o],
               ent_send.at[1, o], ent_recv.at[1, o], (o, m)).wait_recv()
    partner = match_ref[g]
    got = jnp.concatenate(
        [peer_main[partner].astype(f32), unfold(peer_rest[partner].astype(f32), rest)], axis=1)
    tab_wide[pl.ds(0, rows), :] = widen(got).astype(bf16)

    def one_tile(t):
        tail = jnp.dot(
            hot(tail_col[t], rows + hub_rows), tab_wide[...], preferred_element_type=f32
        ).astype(bf16)
        q = query[t]
        scores = lax.dot_general(q, tail, contract_last, preferred_element_type=f32)
        expo = jnp.exp(scores - jnp.max(scores, axis=1, keepdims=True))
        probs = expo * (1.0 / jnp.sum(expo, axis=1, keepdims=True))
        eye = lax.broadcasted_iota(jnp.int32, (edge, edge), 0) == lax.broadcasted_iota(
            jnp.int32, (edge, edge), 1)
        diff = jnp.where(eye, probs - 1.0, probs).astype(bf16)
        dq = jnp.dot(diff, tail, preferred_element_type=f32)
        here = pl.ds(pl.multiple_of(t * edge, edge), edge)
        d_tail[here, :] = lax.dot_general(
            diff, q, contract_first, preferred_element_type=f32).astype(bf16)
        w = weights[pl.ds(t, 1), :]
        wr, wi = w[:, :HALF], w[:, HALF:]
        dr, di = dq[:, :HALF], dq[:, HALF:]
        d_head[here, :] = jnp.concatenate(
            [dr * wr + di * wi, di * wr - dr * wi], axis=1).astype(bf16)

    def tile_pair(i, _):
        one_tile(2 * i)
        one_tile(2 * i + 1)
        return 0

    lax.fori_loop(0, tiles // 2, tile_pair, 0)

    def scatter(ids, low, n, grads):
        hot_t = (ids == lax.broadcasted_iota(jnp.int32, (n, tiles * edge), 0) + low)
        return jnp.dot(hot_t.astype(f32).astype(bf16), grads, preferred_element_type=f32)

    def send_back(part, acc):
        low = part * part_rows
        flat = narrow(acc, half)
        back_main[g, low : low + part_rows, :] = flat[:, :main].astype(bf16)
        back_rest[g, part * part_rest : (part + 1) * part_rest, :] = fold(flat[:, main:]).astype(bf16)
        for copy in back_copies(part, g):
            copy.start()

    def back_copies(part, slot):
        out = []
        a = pl.ds(part * part_rows, part_rows)
        b = pl.ds(part * part_rest, part_rest)
        for o in other_groups:
            at = g if slot is g else o
            out.append(remote(back_main.at[at, a], back_main.at[at, a],
                              back_send.at[part, 0, o], back_recv.at[part, 0, at], (o, m)))
            out.append(remote(back_rest.at[at, b], back_rest.at[at, b],
                              back_send.at[part, 1, o], back_recv.at[part, 1, at], (o, m)))
        return out

    last = parts - 1
    acc = scatter(tail_row[...], last * part_rows, part_rows + hub_rows, d_tail[...])
    hub_acc = acc[part_rows:]
    for c in range(CHUNKS):
        r, k = c // 2 * CHUNK_ROWS, c % 2 * HALF
        hub_send[c] = hub_acc[r : r + CHUNK_ROWS, k : k + HALF].astype(bf16)

    owner = m < CHUNKS

    def stage_one(o):
        return remote(hub_send.at[o], hub_in.at[m], s1.at[o], r1.at[m], (g, o))

    for o in other_members:
        @pl.when(o < CHUNKS)
        def _(o=o):
            stage_one(o).start()

    @pl.when(owner)
    def _():
        hub_in[m] = hub_send[m]

    send_back(last, acc[:part_rows])
    for part in range(last):
        send_back(part, scatter(tail_row[...], part * part_rows, part_rows, d_tail[...]))

    def stage_two(o, at):
        return remote(hub_mid.at[at], hub_mid.at[at], s2.at[o], r2.at[at], (o, m))

    @pl.when(owner)
    def _():
        for o in other_members:
            remote(hub_send.at[m], hub_in.at[o], s1.at[o], r1.at[o], (g, o)).wait_recv()
        total = hub_in[0].astype(f32)
        for i in range(1, members):
            total = total + hub_in[i].astype(f32)
        hub_mid[g] = total
        for o in other_groups:
            stage_two(o, g).start()

    back_sum[...] = scatter(head_row[...], 0, rows, d_head[...])

    def stage_three(o, at):
        return remote(hub_out.at[at], hub_out.at[at], s3.at[o], r3.at[at], (g, o))

    @pl.when(owner)
    def _():
        for o in other_groups:
            stage_two(o, o).wait_recv()
        total = hub_mid[0]
        for i in range(1, groups):
            total = total + hub_mid[i]
        hub_out[m] = (hub_wide[m] - learn_rate * total).astype(bf16)
        for o in other_members:
            stage_three(o, m).start()

    for part in [last, *range(last)]:
        for copy in back_copies(part, None):
            copy.wait_recv()
    source = jnp.int32(0)
    for i in range(1, groups):
        source = jnp.where(match_ref[i] == g, i, source)
    for part in [last, *range(last)]:
        low = part * part_rows
        returned = jnp.concatenate(
            [
                back_main[source, low : low + part_rows, :].astype(f32),
                unfold(back_rest[source, part * part_rest : (part + 1) * part_rest, :].astype(f32), rest),
            ],
            axis=1,
        )
        grads = narrow(back_sum[low : low + part_rows, :], half) + returned
        new_ent_ref[low : low + part_rows, :] = (
            ent_ref[low : low + part_rows, :].astype(f32) - learn_rate * grads).astype(bf16)

    for o in other_members:
        @pl.when(o < CHUNKS)
        def _(o=o):
            stage_three(o, o).wait_recv()
    for r in range(CHUNKS // 2):
        pair = jnp.concatenate([hub_out[2 * r].astype(f32), hub_out[2 * r + 1].astype(f32)], axis=1)
        new_hub_ref[r * CHUNK_ROWS : (r + 1) * CHUNK_ROWS, :] = narrow(pair, half).astype(bf16)

    for copy in sends:
        copy.wait_send()
    for part in range(parts):
        for copy in back_copies(part, g):
            copy.wait_send()
    for o in other_members:
        @pl.when(o < CHUNKS)
        def _(o=o):
            stage_one(o).wait_send()

    @pl.when(owner)
    def _():
        for o in other_groups:
            stage_two(o, g).wait_send()
        for o in other_members:
            stage_three(o, m).wait_send()


def shards(groups, members, entities, hub_rows, relations, matching, head_index, tail_index, tile_rel, tile_count):
    rows, width = entities.shape
    hubs = hub_rows.shape[0]
    tiles, edge = head_index.shape
    main = width // LANES * LANES
    folded = rows * (width - main) // LANES
    parts = 2
    smem = pl.BlockSpec(memory_space=pltpu.SMEM)
    vmem = pl.BlockSpec(memory_space=pltpu.VMEM)
    dma = pltpu.SemaphoreType.DMA
    return pl.pallas_call(
        functools.partial(kernel, groups, members),
        out_shape=(
            jax.ShapeDtypeStruct(entities.shape, bf16),
            jax.ShapeDtypeStruct(hub_rows.shape, bf16),
        ),
        in_specs=[smem, smem, smem, vmem, vmem, vmem, vmem, pl.BlockSpec(memory_space=pl.ANY)],
        out_specs=(vmem, vmem),
        scratch_shapes=[
            pltpu.VMEM(relations.shape, f32),
            pltpu.VMEM((rows, WIDE), bf16),
            pltpu.VMEM((rows + hubs, WIDE), bf16),
            pltpu.VMEM((CHUNKS, CHUNK_ROWS, HALF), f32),
            pltpu.VMEM((groups, rows, main), bf16),
            pltpu.VMEM((groups, folded, LANES), bf16),
            pltpu.VMEM((folded, LANES), bf16),
            pltpu.VMEM((tiles, edge, 1), jnp.int32),
            pltpu.VMEM((tiles, edge, 1), jnp.int32),
            pltpu.VMEM((1, tiles * edge), jnp.int32),
            pltpu.VMEM((1, tiles * edge), jnp.int32),
            pltpu.VMEM((tiles, WIDE), f32),
            pltpu.VMEM((tiles, edge, WIDE), bf16),
            pltpu.VMEM((tiles * edge, WIDE), bf16),
            pltpu.VMEM((tiles * edge, WIDE), bf16),
            pltpu.VMEM((groups, rows, main), bf16),
            pltpu.VMEM((groups, folded, LANES), bf16),
            pltpu.VMEM((rows, WIDE), f32),
            pltpu.VMEM((CHUNKS, CHUNK_ROWS, HALF), bf16),
            pltpu.VMEM((members, CHUNK_ROWS, HALF), bf16),
            pltpu.VMEM((groups, CHUNK_ROWS, HALF), f32),
            pltpu.VMEM((CHUNKS, CHUNK_ROWS, HALF), bf16),
            dma,
            dma((2, groups)),
            dma((2, groups)),
            dma((parts, 2, groups)),
            dma((parts, 2, groups)),
            dma((members,)),
            dma((members,)),
            dma((groups,)),
            dma((groups,)),
            dma((members,)),
            dma((members,)),
        ],
        compiler_params=pltpu.CompilerParams(
            collective_id=0, has_side_effects=True, vmem_limit_bytes=56 * 1024 * 1024
        ),
        cost_estimate=pl.CostEstimate(
            flops=4 * tiles * edge * WIDE * (2 * rows + hubs + edge), bytes_accessed=relations.size * 4,
            transcendentals=tiles * edge * edge),
    )(tile_count, tile_rel, matching, entities, hub_rows, head_index, tail_index, relations)


def solution(mesh):
    placed = (
        P(("group", "member"), None),
        P(),
        P(),
        P(),
        P(("group", "member"), None),
        P(("group", "member"), None),
        P(("group", "member")),
        P("group", "member"),
    )
    return jax.shard_map(
        functools.partial(shards, mesh.shape["group"], mesh.shape["member"]),
        mesh=mesh,
        in_specs=placed,
        out_specs=(P(("group", "member"), None), P()),
        check_vma=False,
    )
```

```python
import functools

import jax
import jax.numpy as jnp
from jax import lax
from jax.experimental import pallas as pl
from jax.experimental.pallas import tpu as pltpu
from jax.sharding import PartitionSpec as P

learn_rate = 0.1
MESH = pl.DeviceIdType.MESH
LANES = 128
CHUNK_ROWS = 32
contract_last = (((1,), (1,)), ((), ()))
f32 = jnp.float32
bf16 = jnp.bfloat16


def dot(a, b):
    return jnp.dot(a, b, preferred_element_type=f32)


def dot_last(a, b):
    return lax.dot_general(a, b, contract_last, preferred_element_type=f32)


def kernel(
    groups, members, count_ref, rel_ref, match_ref,
    ent_ref, hub_ref, head_ref, tail_ref, table_ref,
    new_ent_ref, new_hub_ref,
    landed, relations, peers_0, peers_1, table, weights, hot_head, hot_tail, picked,
    query_t, query, d_head, d_tail, back_0, back_1, head_sum,
    hub_pad, hub_send, hub_in, hub_mid, hub_out,
    rel_sem, ent_send, ent_recv, back_send, back_recv,
    s1, r1, s2, r2, s3, r3,
):
    g = lax.axis_index("group")
    m = lax.axis_index("member")
    width, rows = ent_ref.shape
    half = width // 2
    hubs = hub_ref.shape[1]
    tiles, edge = head_ref.shape
    rels = table_ref.shape[1]
    peers, back = (peers_0, peers_1), (back_0, back_1)
    parts = len(back)
    part_rows = rows // parts
    chunks = hub_send.shape[0]

    blocks = relations.shape[0]
    load = pltpu.make_async_copy(table_ref, landed, rel_sem)
    load.start()
    other_groups = [lax.rem(g + d, groups) for d in range(1, groups)]
    other_members = [lax.rem(m + d, members) for d in range(1, members)]
    barrier = pltpu.get_barrier_semaphore()
    for o in other_groups:
        pl.semaphore_signal(barrier, inc=1, device_id=(o, m), device_id_type=MESH)
    for o in other_members:
        pl.semaphore_signal(barrier, inc=1, device_id=(g, o), device_id_type=MESH)
    pl.semaphore_wait(barrier, groups + members - 2)

    def remote(src, dst, send, recv, where):
        return pltpu.make_async_remote_copy(
            src_ref=src, dst_ref=dst, send_sem=send, recv_sem=recv,
            device_id=where, device_id_type=MESH,
        )

    def lanes_of(part):
        return pl.ds(part * part_rows, part_rows)

    def ent_copy(part, o, slot):
        return remote(ent_ref.at[:, lanes_of(part)], peers[part].at[slot],
                      ent_send.at[part, o], ent_recv.at[part, slot], (o, m))

    for part in range(parts):
        for o in other_groups:
            ent_copy(part, o, g).start()

    for part in range(parts):
        peers[part][g] = ent_ref[:, lanes_of(part)]
    hub_now = hub_ref[...].astype(f32)
    for c in range(chunks):
        piece = hub_now[c * CHUNK_ROWS : (c + 1) * CHUNK_ROWS]
        hub_pad[c, : piece.shape[0], :] = piece
        if piece.shape[0] < CHUNK_ROWS:
            hub_pad[c, piece.shape[0] :, :] = jnp.zeros(
                (CHUNK_ROWS - piece.shape[0], hubs), f32)
    load.wait()
    for i in range(blocks):
        piece = landed[:, i * LANES : (i + 1) * LANES]
        if piece.shape[1] < LANES:
            piece = jnp.concatenate(
                [piece, jnp.zeros((width, LANES - piece.shape[1]), f32)], axis=1)
        relations[i] = piece
    live = count_ref[0, 0]
    lane = lax.broadcasted_iota(jnp.int32, (width, LANES), 1)

    def lanes_at(t):
        return pl.ds(pl.multiple_of(t * edge, edge), edge)

    def hot(ids, n):
        return (lax.broadcasted_iota(jnp.int32, (n, edge), 0) == ids).astype(f32).astype(bf16)

    def weight_of(t):
        rel = rel_ref[t]
        block = jnp.int32(0)
        for i in range(1, blocks):
            block = jnp.where(rel >= i * LANES, i, block)
        kept = jnp.where(lane == rel - block * LANES, relations[block], 0.0)
        column = jnp.sum(kept, axis=1, keepdims=True)
        column = jnp.where(t < live, column, jnp.zeros_like(column))
        weights[t] = jnp.broadcast_to(column, (width, LANES))

    def halves(t):
        w = jnp.concatenate([weights[t]] * (edge // LANES), axis=1)
        return w[:half], w[half:]

    def prepare(t):
        at = lanes_at(t)
        hot_h = hot(head_ref[pl.ds(t, 1), :], rows)
        hot_head[:, at] = hot_h
        head = dot(ent_ref[...], hot_h)
        wr, wi = halves(t)
        hr, hi = head[:half], head[half:]
        q = jnp.concatenate([hr * wr - hi * wi, hr * wi + hi * wr], axis=0)
        query_t[:, at] = q.astype(bf16)
        query[t] = q.T.astype(bf16)
        hot_t = hot(tail_ref[pl.ds(t, 1), :], rows + hubs)
        hot_tail[:, at] = hot_t
        picked[:, at] = dot(hub_ref[...], hot_t[rows:]).astype(bf16)

    def pairs(step):
        def body(i, _):
            step(2 * i)
            step(2 * i + 1)
            return 0

        lax.fori_loop(0, tiles // 2, body, 0)

    for t in range(tiles):
        weight_of(t)
    pairs(prepare)

    def wait_rows(part):
        for o in other_groups:
            ent_copy(part, o, o).wait_recv()
        table[:, lanes_of(part)] = peers[part][partner]

    partner = match_ref[g]

    def pick(part, t):
        at = lanes_at(t)
        found = dot(table[:, lanes_of(part)], hot_tail[lanes_of(part), at])
        return (found + picked[:, at].astype(f32)).astype(bf16)

    for part in range(parts - 1):
        wait_rows(part)

        def add_part(t, part=part):
            picked[:, lanes_at(t)] = pick(part, t)

        pairs(add_part)
    wait_rows(parts - 1)

    def one_tile(t):
        at = lanes_at(t)
        tail = pick(parts - 1, t)
        scores = dot(query[t], tail)
        expo = jnp.exp(scores - jnp.max(scores, axis=1, keepdims=True))
        probs = expo * (1.0 / jnp.sum(expo, axis=1, keepdims=True))
        eye = lax.broadcasted_iota(jnp.int32, (edge, edge), 0) == lax.broadcasted_iota(
            jnp.int32, (edge, edge), 1)
        diff = jnp.where(eye, probs - 1.0, probs).astype(bf16)
        d_tail[:, at] = dot(query_t[:, at], diff).astype(bf16)
        dq = dot_last(tail, diff)
        wr, wi = halves(t)
        dr, di = dq[:half], dq[half:]
        d_head[:, at] = jnp.concatenate(
            [dr * wr + di * wi, di * wr - dr * wi], axis=0).astype(bf16)

    pairs(one_tile)

    def back_copy(part, o, slot):
        return remote(back[part].at[slot], back[part].at[slot],
                      back_send.at[part, o], back_recv.at[part, slot], (o, m))

    def send_back(part, acc):
        back[part][g] = acc.astype(bf16)
        for o in other_groups:
            back_copy(part, o, g).start()

    last = parts - 1
    acc = dot_last(d_tail[...], hot_tail[last * part_rows :, :])
    send_back(last, acc[:, :part_rows])
    for c in range(chunks):
        piece = acc[c * CHUNK_ROWS : (c + 1) * CHUNK_ROWS, part_rows:]
        if piece.shape[0] < CHUNK_ROWS:
            piece = jnp.concatenate(
                [piece, jnp.zeros((CHUNK_ROWS - piece.shape[0], hubs), f32)], axis=0)
        hub_send[c] = piece.astype(bf16)

    owner = m < chunks

    for o in other_members:
        @pl.when(o < chunks)
        def _(o=o):
            remote(hub_send.at[o], hub_in.at[m], s1.at[o], r1.at[m], (g, o)).start()

    @pl.when(owner)
    def _():
        hub_in[m] = hub_send[m]

    for part in range(last):
        send_back(part, dot_last(d_tail[...], hot_tail[lanes_of(part), :]))

    def stage_two(o, slot):
        return remote(hub_mid.at[slot], hub_mid.at[slot], s2.at[o], r2.at[slot], (o, m))

    @pl.when(owner)
    def _():
        for o in other_members:
            remote(hub_send.at[m], hub_in.at[o], s1.at[o], r1.at[o], (g, o)).wait_recv()
        total = hub_in[0].astype(f32)
        for i in range(1, members):
            total = total + hub_in[i].astype(f32)
        hub_mid[g] = total
        for o in other_groups:
            stage_two(o, g).start()

    head_sum[...] = dot_last(d_head[...], hot_head[...])

    def stage_three(o, slot):
        return remote(hub_out.at[slot], hub_out.at[slot], s3.at[o], r3.at[slot], (g, o))

    @pl.when(owner)
    def _():
        for o in other_groups:
            stage_two(o, o).wait_recv()
        total = hub_mid[0]
        for i in range(1, groups):
            total = total + hub_mid[i]
        hub_out[m] = (hub_pad[m] - learn_rate * total).astype(bf16)
        for o in other_members:
            stage_three(o, m).start()

    source = jnp.int32(0)
    for i in range(1, groups):
        source = jnp.where(match_ref[i] == g, i, source)
    for part in [last, *range(last)]:
        for o in other_groups:
            back_copy(part, o, o).wait_recv()
        at = lanes_of(part)
        grads = head_sum[:, at] + back[part][source].astype(f32)
        new_ent_ref[:, at] = (ent_ref[:, at].astype(f32) - learn_rate * grads).astype(bf16)

    for o in other_members:
        @pl.when(o < chunks)
        def _(o=o):
            stage_three(o, o).wait_recv()
    new_hub_ref[...] = hub_out[...].reshape(chunks * CHUNK_ROWS, hubs)[:width]

    for part in range(parts):
        for o in other_groups:
            ent_copy(part, o, g).wait_send()
            back_copy(part, o, g).wait_send()
    for o in other_members:
        @pl.when(o < chunks)
        def _(o=o):
            remote(hub_send.at[o], hub_in.at[m], s1.at[o], r1.at[m], (g, o)).wait_send()

    @pl.when(owner)
    def _():
        for o in other_groups:
            stage_two(o, g).wait_send()
        for o in other_members:
            stage_three(o, m).wait_send()


def shards(groups, members, entities, hub_rows, relations, matching, head_index, tail_index, tile_rel, tile_count):
    rows, width = entities.shape
    hubs = hub_rows.shape[0]
    tiles, edge = head_index.shape
    edges = tiles * edge
    chunks = -(-width // CHUNK_ROWS)
    blocks = -(-relations.shape[0] // LANES)
    parts = 2
    smem = pl.BlockSpec(memory_space=pltpu.SMEM)
    vmem = pl.BlockSpec(memory_space=pltpu.VMEM)
    dma = pltpu.SemaphoreType.DMA
    new_ent, new_hub = pl.pallas_call(
        functools.partial(kernel, groups, members),
        out_shape=(
            jax.ShapeDtypeStruct((width, rows), bf16),
            jax.ShapeDtypeStruct((width, hubs), bf16),
        ),
        in_specs=[smem, smem, smem, vmem, vmem, vmem, vmem, pl.BlockSpec(memory_space=pl.ANY)],
        out_specs=(vmem, vmem),
        scratch_shapes=[
            pltpu.VMEM((width, relations.shape[0]), f32),
            pltpu.VMEM((blocks, width, LANES), f32),
            pltpu.VMEM((groups, width, rows // parts), bf16),
            pltpu.VMEM((groups, width, rows // parts), bf16),
            pltpu.VMEM((width, rows), bf16),
            pltpu.VMEM((tiles, width, LANES), f32),
            pltpu.VMEM((rows, edges), bf16),
            pltpu.VMEM((rows + hubs, edges), bf16),
            pltpu.VMEM((width, edges), bf16),
            pltpu.VMEM((width, edges), bf16),
            pltpu.VMEM((tiles, edge, width), bf16),
            pltpu.VMEM((width, edges), bf16),
            pltpu.VMEM((width, edges), bf16),
            pltpu.VMEM((groups, width, rows // parts), bf16),
            pltpu.VMEM((groups, width, rows // parts), bf16),
            pltpu.VMEM((width, rows), f32),
            pltpu.VMEM((chunks, CHUNK_ROWS, hubs), f32),
            pltpu.VMEM((chunks, CHUNK_ROWS, hubs), bf16),
            pltpu.VMEM((members, CHUNK_ROWS, hubs), bf16),
            pltpu.VMEM((groups, CHUNK_ROWS, hubs), f32),
            pltpu.VMEM((chunks, CHUNK_ROWS, hubs), bf16),
            dma,
            dma((parts, groups)),
            dma((parts, groups)),
            dma((parts, groups)),
            dma((parts, groups)),
            dma((members,)),
            dma((members,)),
            dma((groups,)),
            dma((groups,)),
            dma((members,)),
            dma((members,)),
        ],
        compiler_params=pltpu.CompilerParams(
            collective_id=0, has_side_effects=True, vmem_limit_bytes=58 * 1024 * 1024
        ),
        cost_estimate=pl.CostEstimate(
            flops=4 * edges * width * (2 * rows + hubs + edge),
            bytes_accessed=relations.size * 4,
            transcendentals=edges * edge),
    )(tile_count, tile_rel, matching, entities.T, hub_rows.T, head_index, tail_index, relations.T)
    return new_ent.T, new_hub.T


def solution(mesh):
    placed = (
        P(("group", "member"), None),
        P(),
        P(),
        P(),
        P(("group", "member"), None),
        P(("group", "member"), None),
        P(("group", "member")),
        P("group", "member"),
    )
    return jax.shard_map(
        functools.partial(shards, mesh.shape["group"], mesh.shape["member"]),
        mesh=mesh,
        in_specs=placed,
        out_specs=(P(("group", "member"), None), P()),
        check_vma=False,
    )
```

```python
import functools

import jax
import jax.numpy as jnp
from jax import lax
from jax.experimental import pallas as pl
from jax.experimental.pallas import tpu as pltpu
from jax.sharding import PartitionSpec as P

learn_rate = 0.1
MESH = pl.DeviceIdType.MESH
LANES = 128
CHUNK_ROWS = 32
UNROLL = 4
contract_last = (((1,), (1,)), ((), ()))
f32 = jnp.float32
bf16 = jnp.bfloat16


def dot(a, b):
    return jnp.dot(a, b, preferred_element_type=f32)


def dot_last(a, b):
    return lax.dot_general(a, b, contract_last, preferred_element_type=f32)


def kernel(
    groups, members, count_ref, rel_ref, match_ref,
    ent_ref, hub_ref, head_ref, tail_ref, table_ref,
    new_ent_ref, new_hub_ref,
    landed, relations, peers_0, peers_1, table, weights, hot_head, hot_tail, picked,
    query_t, query, d_head, d_tail, back_0, back_1, head_sum,
    hub_pad, hub_send, hub_in, hub_mid, hub_out,
    rel_sem, ent_send, ent_recv, back_send, back_recv,
    s1, r1, s2, r2, s3, r3,
):
    g = lax.axis_index("group")
    m = lax.axis_index("member")
    width, rows = ent_ref.shape
    half = width // 2
    hubs = hub_ref.shape[1]
    tiles, edge = head_ref.shape
    rels = table_ref.shape[1]
    peers, back = (peers_0, peers_1), (back_0, back_1)
    parts = len(back)
    part_rows = rows // parts
    chunks = hub_send.shape[0]

    blocks = relations.shape[0]
    load = pltpu.make_async_copy(table_ref, landed, rel_sem)
    load.start()
    other_groups = [lax.rem(g + d, groups) for d in range(1, groups)]
    other_members = [lax.rem(m + d, members) for d in range(1, members)]
    barrier = pltpu.get_barrier_semaphore()
    for o in other_groups:
        pl.semaphore_signal(barrier, inc=1, device_id=(o, m), device_id_type=MESH)
    for o in other_members:
        pl.semaphore_signal(barrier, inc=1, device_id=(g, o), device_id_type=MESH)
    pl.semaphore_wait(barrier, groups + members - 2)

    def remote(src, dst, send, recv, where):
        return pltpu.make_async_remote_copy(
            src_ref=src, dst_ref=dst, send_sem=send, recv_sem=recv,
            device_id=where, device_id_type=MESH,
        )

    def lanes_of(part):
        return pl.ds(part * part_rows, part_rows)

    def ent_copy(part, o, slot):
        return remote(ent_ref.at[:, lanes_of(part)], peers[part].at[slot],
                      ent_send.at[part, o], ent_recv.at[part, slot], (o, m))

    for part in range(parts):
        for o in other_groups:
            ent_copy(part, o, g).start()

    for part in range(parts):
        peers[part][g] = ent_ref[:, lanes_of(part)]
    hub_now = hub_ref[...].astype(f32)
    for c in range(chunks):
        piece = hub_now[c * CHUNK_ROWS : (c + 1) * CHUNK_ROWS]
        hub_pad[c, : piece.shape[0], :] = piece
        if piece.shape[0] < CHUNK_ROWS:
            hub_pad[c, piece.shape[0] :, :] = jnp.zeros(
                (CHUNK_ROWS - piece.shape[0], hubs), f32)
    load.wait()
    for i in range(blocks):
        piece = landed[:, i * LANES : (i + 1) * LANES]
        if piece.shape[1] < LANES:
            piece = jnp.concatenate(
                [piece, jnp.zeros((width, LANES - piece.shape[1]), f32)], axis=1)
        relations[i] = piece
    live = count_ref[0, 0]
    lane = lax.broadcasted_iota(jnp.int32, (width, LANES), 1)

    def lanes_at(t):
        return pl.ds(pl.multiple_of(t * edge, edge), edge)

    def hot(ids, n):
        return (lax.broadcasted_iota(jnp.int32, (n, edge), 0) == ids).astype(f32).astype(bf16)

    def weight_of(t):
        rel = rel_ref[t]
        block = jnp.int32(0)
        for i in range(1, blocks):
            block = jnp.where(rel >= i * LANES, i, block)
        kept = jnp.where(lane == rel - block * LANES, relations[block], 0.0)
        column = jnp.sum(kept, axis=1, keepdims=True)
        column = jnp.where(t < live, column, jnp.zeros_like(column))
        weights[t] = jnp.broadcast_to(column, (width, LANES))

    def halves(t):
        w = jnp.concatenate([weights[t]] * (edge // LANES), axis=1)
        return w[:half], w[half:]

    def prepare(t):
        at = lanes_at(t)
        hot_h = hot(head_ref[pl.ds(t, 1), :], rows)
        hot_head[:, at] = hot_h
        head = dot(ent_ref[...], hot_h)
        wr, wi = halves(t)
        hr, hi = head[:half], head[half:]
        q = jnp.concatenate([hr * wr - hi * wi, hr * wi + hi * wr], axis=0)
        query_t[:, at] = q.astype(bf16)
        query[t] = q.T.astype(bf16)
        hot_t = hot(tail_ref[pl.ds(t, 1), :], rows + hubs)
        hot_tail[:, at] = hot_t
        picked[:, at] = dot(hub_ref[...], hot_t[rows:]).astype(bf16)

    def quads(step):
        def body(i, _):
            for k in range(UNROLL):
                step(UNROLL * i + k)
            return 0

        lax.fori_loop(0, tiles // UNROLL, body, 0)

    for t in range(tiles):
        weight_of(t)
    quads(prepare)

    def wait_rows(part):
        for o in other_groups:
            ent_copy(part, o, o).wait_recv()
        table[:, lanes_of(part)] = peers[part][partner]

    partner = match_ref[g]

    def pick(part, t):
        at = lanes_at(t)
        found = dot(table[:, lanes_of(part)], hot_tail[lanes_of(part), at])
        return (found + picked[:, at].astype(f32)).astype(bf16)

    for part in range(parts - 1):
        wait_rows(part)

        def add_part(t, part=part):
            picked[:, lanes_at(t)] = pick(part, t)

        quads(add_part)
    wait_rows(parts - 1)

    def one_tile(t):
        at = lanes_at(t)
        tail = pick(parts - 1, t)
        scores = dot(query[t], tail)
        expo = jnp.exp(scores - jnp.max(scores, axis=1, keepdims=True))
        probs = expo * (1.0 / jnp.sum(expo, axis=1, keepdims=True))
        eye = lax.broadcasted_iota(jnp.int32, (edge, edge), 0) == lax.broadcasted_iota(
            jnp.int32, (edge, edge), 1)
        diff = jnp.where(eye, probs - 1.0, probs).astype(bf16)
        d_tail[:, at] = dot(query_t[:, at], diff).astype(bf16)
        dq = dot_last(tail, diff)
        wr, wi = halves(t)
        dr, di = dq[:half], dq[half:]
        d_head[:, at] = jnp.concatenate(
            [dr * wr + di * wi, di * wr - dr * wi], axis=0).astype(bf16)

    quads(one_tile)

    def back_copy(part, o, slot):
        return remote(back[part].at[slot], back[part].at[slot],
                      back_send.at[part, o], back_recv.at[part, slot], (o, m))

    def send_back(part, acc):
        back[part][g] = acc.astype(bf16)
        for o in other_groups:
            back_copy(part, o, g).start()

    last = parts - 1
    acc = dot_last(d_tail[...], hot_tail[last * part_rows :, :])
    send_back(last, acc[:, :part_rows])
    for c in range(chunks):
        piece = acc[c * CHUNK_ROWS : (c + 1) * CHUNK_ROWS, part_rows:]
        if piece.shape[0] < CHUNK_ROWS:
            piece = jnp.concatenate(
                [piece, jnp.zeros((CHUNK_ROWS - piece.shape[0], hubs), f32)], axis=0)
        hub_send[c] = piece.astype(bf16)

    owner = m < chunks

    for o in other_members:
        @pl.when(o < chunks)
        def _(o=o):
            remote(hub_send.at[o], hub_in.at[m], s1.at[o], r1.at[m], (g, o)).start()

    @pl.when(owner)
    def _():
        hub_in[m] = hub_send[m]

    for part in range(last):
        send_back(part, dot_last(d_tail[...], hot_tail[lanes_of(part), :]))

    def stage_two(o, slot):
        return remote(hub_mid.at[slot], hub_mid.at[slot], s2.at[o], r2.at[slot], (o, m))

    @pl.when(owner)
    def _():
        for o in other_members:
            remote(hub_send.at[m], hub_in.at[o], s1.at[o], r1.at[o], (g, o)).wait_recv()
        total = hub_in[0].astype(f32)
        for i in range(1, members):
            total = total + hub_in[i].astype(f32)
        hub_mid[g] = total
        for o in other_groups:
            stage_two(o, g).start()

    head_sum[...] = dot_last(d_head[...], hot_head[...])

    def stage_three(o, slot):
        return remote(hub_out.at[slot], hub_out.at[slot], s3.at[o], r3.at[slot], (g, o))

    @pl.when(owner)
    def _():
        for o in other_groups:
            stage_two(o, o).wait_recv()
        total = hub_mid[0]
        for i in range(1, groups):
            total = total + hub_mid[i]
        hub_out[m] = (hub_pad[m] - learn_rate * total).astype(bf16)
        for o in other_members:
            stage_three(o, m).start()

    source = jnp.int32(0)
    for i in range(1, groups):
        source = jnp.where(match_ref[i] == g, i, source)
    for part in [last, *range(last)]:
        for o in other_groups:
            back_copy(part, o, o).wait_recv()
        at = lanes_of(part)
        grads = head_sum[:, at] + back[part][source].astype(f32)
        new_ent_ref[:, at] = (ent_ref[:, at].astype(f32) - learn_rate * grads).astype(bf16)

    for o in other_members:
        @pl.when(o < chunks)
        def _(o=o):
            stage_three(o, o).wait_recv()
    new_hub_ref[...] = hub_out[...].reshape(chunks * CHUNK_ROWS, hubs)[:width]

    for part in range(parts):
        for o in other_groups:
            ent_copy(part, o, g).wait_send()
            back_copy(part, o, g).wait_send()
    for o in other_members:
        @pl.when(o < chunks)
        def _(o=o):
            remote(hub_send.at[o], hub_in.at[m], s1.at[o], r1.at[m], (g, o)).wait_send()

    @pl.when(owner)
    def _():
        for o in other_groups:
            stage_two(o, g).wait_send()
        for o in other_members:
            stage_three(o, m).wait_send()


def hand_over(ent_ref, hub_ref, new_ent_ref, new_hub_ref):
    new_ent_ref[...] = ent_ref[...]
    new_hub_ref[...] = hub_ref[...]


def shards(groups, members, entities, hub_rows, relations, matching, head_index, tail_index, tile_rel, tile_count):
    rows, width = entities.shape
    hubs = hub_rows.shape[0]
    tiles, edge = head_index.shape
    edges = tiles * edge
    chunks = -(-width // CHUNK_ROWS)
    blocks = -(-relations.shape[0] // LANES)
    parts = 2
    smem = pl.BlockSpec(memory_space=pltpu.SMEM)
    vmem = pl.BlockSpec(memory_space=pltpu.VMEM)
    dma = pltpu.SemaphoreType.DMA
    new_ent, new_hub = pl.pallas_call(
        functools.partial(kernel, groups, members),
        out_shape=(
            jax.ShapeDtypeStruct((width, rows), bf16),
            jax.ShapeDtypeStruct((width, hubs), bf16),
        ),
        in_specs=[smem, smem, smem, vmem, vmem, vmem, vmem, pl.BlockSpec(memory_space=pl.ANY)],
        out_specs=(vmem, vmem),
        scratch_shapes=[
            pltpu.VMEM((width, relations.shape[0]), f32),
            pltpu.VMEM((blocks, width, LANES), f32),
            pltpu.VMEM((groups, width, rows // parts), bf16),
            pltpu.VMEM((groups, width, rows // parts), bf16),
            pltpu.VMEM((width, rows), bf16),
            pltpu.VMEM((tiles, width, LANES), f32),
            pltpu.VMEM((rows, edges), bf16),
            pltpu.VMEM((rows + hubs, edges), bf16),
            pltpu.VMEM((width, edges), bf16),
            pltpu.VMEM((width, edges), bf16),
            pltpu.VMEM((tiles, edge, width), bf16),
            pltpu.VMEM((width, edges), bf16),
            pltpu.VMEM((width, edges), bf16),
            pltpu.VMEM((groups, width, rows // parts), bf16),
            pltpu.VMEM((groups, width, rows // parts), bf16),
            pltpu.VMEM((width, rows), f32),
            pltpu.VMEM((chunks, CHUNK_ROWS, hubs), f32),
            pltpu.VMEM((chunks, CHUNK_ROWS, hubs), bf16),
            pltpu.VMEM((members, CHUNK_ROWS, hubs), bf16),
            pltpu.VMEM((groups, CHUNK_ROWS, hubs), f32),
            pltpu.VMEM((chunks, CHUNK_ROWS, hubs), bf16),
            dma,
            dma((parts, groups)),
            dma((parts, groups)),
            dma((parts, groups)),
            dma((parts, groups)),
            dma((members,)),
            dma((members,)),
            dma((groups,)),
            dma((groups,)),
            dma((members,)),
            dma((members,)),
        ],
        compiler_params=pltpu.CompilerParams(
            collective_id=0, has_side_effects=True, vmem_limit_bytes=58 * 1024 * 1024
        ),
        cost_estimate=pl.CostEstimate(
            flops=4 * edges * width * (2 * rows + hubs + edge),
            bytes_accessed=relations.size * 4,
            transcendentals=edges * edge),
    )(tile_count, tile_rel, matching, entities.T, hub_rows.T, head_index, tail_index, relations.T)
    new_ent, new_hub = pl.pallas_call(
        hand_over,
        out_shape=(
            jax.ShapeDtypeStruct(new_ent.shape, bf16),
            jax.ShapeDtypeStruct(new_hub.shape, bf16),
        ),
        in_specs=[vmem, vmem],
        out_specs=(vmem, vmem),
    )(new_ent, new_hub)
    return new_ent.T, new_hub.T


def solution(mesh):
    placed = (
        P(("group", "member"), None),
        P(),
        P(),
        P(),
        P(("group", "member"), None),
        P(("group", "member"), None),
        P(("group", "member")),
        P("group", "member"),
    )
    return jax.shard_map(
        functools.partial(shards, mesh.shape["group"], mesh.shape["member"]),
        mesh=mesh,
        in_specs=placed,
        out_specs=(P(("group", "member"), None), P()),
        check_vma=False,
    )
```

```python
import functools

import jax
import jax.numpy as jnp
from jax import lax
from jax.experimental import pallas as pl
from jax.experimental.pallas import tpu as pltpu
from jax.sharding import PartitionSpec as P

learn_rate = 0.1
MESH = pl.DeviceIdType.MESH
LANES = 128
CHUNK_ROWS = 32
UNROLL = 4
contract_last = (((1,), (1,)), ((), ()))
f32 = jnp.float32
bf16 = jnp.bfloat16


def dot(a, b):
    return jnp.dot(a, b, preferred_element_type=f32)


def dot_last(a, b):
    return lax.dot_general(a, b, contract_last, preferred_element_type=f32)


def kernel(
    groups, members, count_ref, rel_ref, match_ref,
    ent_ref, hub_ref, head_ref, tail_ref, table_ref,
    new_ent_ref, new_hub_ref,
    landed, relations, peers_0, peers_1, table, weights, hot_head, hot_tail, picked,
    query_t, query, d_head, d_tail, back_0, back_1, head_sum,
    scores_0, scores_1, diff_0, diff_1,
    hub_pad, hub_send, hub_in, hub_mid, hub_out,
    rel_sem, ent_send, ent_recv, back_send, back_recv,
    s1, r1, s2, r2, s3, r3,
):
    g = lax.axis_index("group")
    m = lax.axis_index("member")
    width, rows = ent_ref.shape
    half = width // 2
    hubs = hub_ref.shape[1]
    tiles, edge = head_ref.shape
    rels = table_ref.shape[1]
    peers, back = (peers_0, peers_1), (back_0, back_1)
    scores_of, diff_of = (scores_0, scores_1), (diff_0, diff_1)
    parts = len(back)
    part_rows = rows // parts
    chunks = hub_send.shape[0]

    blocks = relations.shape[0]
    load = pltpu.make_async_copy(table_ref, landed, rel_sem)
    load.start()
    other_groups = [lax.rem(g + d, groups) for d in range(1, groups)]
    other_members = [lax.rem(m + d, members) for d in range(1, members)]
    barrier = pltpu.get_barrier_semaphore()
    for o in other_groups:
        pl.semaphore_signal(barrier, inc=1, device_id=(o, m), device_id_type=MESH)
    for o in other_members:
        pl.semaphore_signal(barrier, inc=1, device_id=(g, o), device_id_type=MESH)
    pl.semaphore_wait(barrier, groups + members - 2)

    def remote(src, dst, send, recv, where):
        return pltpu.make_async_remote_copy(
            src_ref=src, dst_ref=dst, send_sem=send, recv_sem=recv,
            device_id=where, device_id_type=MESH,
        )

    def lanes_of(part):
        return pl.ds(part * part_rows, part_rows)

    def ent_copy(part, o, slot):
        return remote(ent_ref.at[:, lanes_of(part)], peers[part].at[slot],
                      ent_send.at[part, o], ent_recv.at[part, slot], (o, m))

    for part in range(parts):
        for o in other_groups:
            ent_copy(part, o, g).start()

    for part in range(parts):
        peers[part][g] = ent_ref[:, lanes_of(part)]
    hub_now = hub_ref[...].astype(f32)
    for c in range(chunks):
        piece = hub_now[c * CHUNK_ROWS : (c + 1) * CHUNK_ROWS]
        hub_pad[c, : piece.shape[0], :] = piece
        if piece.shape[0] < CHUNK_ROWS:
            hub_pad[c, piece.shape[0] :, :] = jnp.zeros(
                (CHUNK_ROWS - piece.shape[0], hubs), f32)
    load.wait()
    for i in range(blocks):
        piece = landed[:, i * LANES : (i + 1) * LANES]
        if piece.shape[1] < LANES:
            piece = jnp.concatenate(
                [piece, jnp.zeros((width, LANES - piece.shape[1]), f32)], axis=1)
        relations[i] = piece
    live = count_ref[0, 0]
    lane = lax.broadcasted_iota(jnp.int32, (width, LANES), 1)

    def lanes_at(t):
        return pl.ds(pl.multiple_of(t * edge, edge), edge)

    def wide_at(t):
        return pl.ds(pl.multiple_of(t * edge, UNROLL * edge), UNROLL * edge)

    def hot(ids, n):
        return (lax.broadcasted_iota(jnp.int32, (n, edge), 0) == ids).astype(f32).astype(bf16)

    def weight_of(t):
        rel = rel_ref[t]
        block = jnp.int32(0)
        for i in range(1, blocks):
            block = jnp.where(rel >= i * LANES, i, block)
        kept = jnp.where(lane == rel - block * LANES, relations[block], 0.0)
        column = jnp.sum(kept, axis=1, keepdims=True)
        column = jnp.where(t < live, column, jnp.zeros_like(column))
        weights[t] = jnp.broadcast_to(column, (width, LANES))

    def halves(t):
        w = jnp.concatenate([weights[t]] * (edge // LANES), axis=1)
        return w[:half], w[half:]

    def prepare(first):
        group = [first + k for k in range(UNROLL)]
        for t in group:
            hot_head[:, lanes_at(t)] = hot(head_ref[pl.ds(t, 1), :], rows)
        found = [dot(ent_ref[...], hot_head[:, lanes_at(t)]) for t in group]
        for t in group:
            hot_tail[:, lanes_at(t)] = hot(tail_ref[pl.ds(t, 1), :], rows + hubs)
        queries = []
        for t, head in zip(group, found):
            wr, wi = halves(t)
            hr, hi = head[:half], head[half:]
            q = jnp.concatenate([hr * wr - hi * wi, hr * wi + hi * wr], axis=0)
            query_t[:, lanes_at(t)] = q.astype(bf16)
            queries.append(q)
        for t, q in zip(group, queries):
            query[t] = q.T.astype(bf16)
        at = wide_at(first)
        picked[:, at] = dot(hub_ref[...], hot_tail[rows:, at]).astype(bf16)

    def quads(step):
        def body(i, _):
            step(UNROLL * i)
            return 0

        lax.fori_loop(0, tiles // UNROLL, body, 0)

    for t in range(tiles):
        weight_of(t)
    quads(prepare)

    def wait_rows(part):
        for o in other_groups:
            ent_copy(part, o, o).wait_recv()
        table[:, lanes_of(part)] = peers[part][partner]

    partner = match_ref[g]

    for part in range(parts):
        wait_rows(part)

        def add_part(first, part=part):
            at = wide_at(first)
            found = dot(table[:, lanes_of(part)], hot_tail[lanes_of(part), at])
            picked[:, at] = (found + picked[:, at].astype(f32)).astype(bf16)

        quads(add_part)

    def make_scores(t, par):
        scores_of[par][...] = dot(query[t], picked[:, lanes_at(t)])

    def make_diff(par):
        scores = scores_of[par][...]
        expo = jnp.exp(scores - jnp.max(scores, axis=1, keepdims=True))
        probs = expo * (1.0 / jnp.sum(expo, axis=1, keepdims=True))
        eye = lax.broadcasted_iota(jnp.int32, (edge, edge), 0) == lax.broadcasted_iota(
            jnp.int32, (edge, edge), 1)
        diff_of[par][...] = jnp.where(eye, probs - 1.0, probs).astype(bf16)

    def make_grads(t, par):
        at = lanes_at(t)
        diff = diff_of[par][...]
        d_tail[:, at] = dot(query_t[:, at], diff).astype(bf16)
        dq = dot_last(picked[:, at], diff)
        wr, wi = halves(t)
        dr, di = dq[:half], dq[half:]
        d_head[:, at] = jnp.concatenate(
            [dr * wr + di * wi, di * wr - dr * wi], axis=0).astype(bf16)

    def two_steps(i, _):
        for par in range(2):
            t = 2 * i + par
            make_scores(t, par)
            make_diff(1 - par)
            make_grads(t - 2, par)
        return 0

    make_scores(0, 0)
    make_scores(1, 1)
    make_diff(0)
    lax.fori_loop(1, tiles // 2, two_steps, 0)
    make_diff(1)
    make_grads(tiles - 2, 0)
    make_grads(tiles - 1, 1)

    def back_copy(part, o, slot):
        return remote(back[part].at[slot], back[part].at[slot],
                      back_send.at[part, o], back_recv.at[part, slot], (o, m))

    def send_back(part, acc):
        back[part][g] = acc.astype(bf16)
        for o in other_groups:
            back_copy(part, o, g).start()

    last = parts - 1
    acc = dot_last(d_tail[...], hot_tail[last * part_rows :, :])
    send_back(last, acc[:, :part_rows])
    for c in range(chunks):
        piece = acc[c * CHUNK_ROWS : (c + 1) * CHUNK_ROWS, part_rows:]
        if piece.shape[0] < CHUNK_ROWS:
            piece = jnp.concatenate(
                [piece, jnp.zeros((CHUNK_ROWS - piece.shape[0], hubs), f32)], axis=0)
        hub_send[c] = piece.astype(bf16)

    owner = m < chunks

    for o in other_members:
        @pl.when(o < chunks)
        def _(o=o):
            remote(hub_send.at[o], hub_in.at[m], s1.at[o], r1.at[m], (g, o)).start()

    @pl.when(owner)
    def _():
        hub_in[m] = hub_send[m]

    for part in range(last):
        send_back(part, dot_last(d_tail[...], hot_tail[lanes_of(part), :]))

    def stage_two(o, slot):
        return remote(hub_mid.at[slot], hub_mid.at[slot], s2.at[o], r2.at[slot], (o, m))

    @pl.when(owner)
    def _():
        for o in other_members:
            remote(hub_send.at[m], hub_in.at[o], s1.at[o], r1.at[o], (g, o)).wait_recv()
        total = hub_in[0].astype(f32)
        for i in range(1, members):
            total = total + hub_in[i].astype(f32)
        hub_mid[g] = total
        for o in other_groups:
            stage_two(o, g).start()

    head_sum[...] = dot_last(d_head[...], hot_head[...])

    def stage_three(o, slot):
        return remote(hub_out.at[slot], hub_out.at[slot], s3.at[o], r3.at[slot], (g, o))

    @pl.when(owner)
    def _():
        for o in other_groups:
            stage_two(o, o).wait_recv()
        total = hub_mid[0]
        for i in range(1, groups):
            total = total + hub_mid[i]
        hub_out[m] = (hub_pad[m] - learn_rate * total).astype(bf16)
        for o in other_members:
            stage_three(o, m).start()

    source = jnp.int32(0)
    for i in range(1, groups):
        source = jnp.where(match_ref[i] == g, i, source)
    for part in [last, *range(last)]:
        for o in other_groups:
            back_copy(part, o, o).wait_recv()
        at = lanes_of(part)
        grads = head_sum[:, at] + back[part][source].astype(f32)
        new_ent_ref[:, at] = (ent_ref[:, at].astype(f32) - learn_rate * grads).astype(bf16)

    for o in other_members:
        @pl.when(o < chunks)
        def _(o=o):
            stage_three(o, o).wait_recv()
    new_hub_ref[...] = hub_out[...].reshape(chunks * CHUNK_ROWS, hubs)[:width]

    for part in range(parts):
        for o in other_groups:
            ent_copy(part, o, g).wait_send()
            back_copy(part, o, g).wait_send()
    for o in other_members:
        @pl.when(o < chunks)
        def _(o=o):
            remote(hub_send.at[o], hub_in.at[m], s1.at[o], r1.at[m], (g, o)).wait_send()

    @pl.when(owner)
    def _():
        for o in other_groups:
            stage_two(o, g).wait_send()
        for o in other_members:
            stage_three(o, m).wait_send()


def hand_over(ent_ref, hub_ref, new_ent_ref, new_hub_ref):
    new_ent_ref[...] = ent_ref[...]
    new_hub_ref[...] = hub_ref[...]


def shards(groups, members, entities, hub_rows, relations, matching, head_index, tail_index, tile_rel, tile_count):
    rows, width = entities.shape
    hubs = hub_rows.shape[0]
    tiles, edge = head_index.shape
    edges = tiles * edge
    chunks = -(-width // CHUNK_ROWS)
    blocks = -(-relations.shape[0] // LANES)
    parts = 2
    smem = pl.BlockSpec(memory_space=pltpu.SMEM)
    vmem = pl.BlockSpec(memory_space=pltpu.VMEM)
    dma = pltpu.SemaphoreType.DMA
    new_ent, new_hub = pl.pallas_call(
        functools.partial(kernel, groups, members),
        out_shape=(
            jax.ShapeDtypeStruct((width, rows), bf16),
            jax.ShapeDtypeStruct((width, hubs), bf16),
        ),
        in_specs=[smem, smem, smem, vmem, vmem, vmem, vmem, pl.BlockSpec(memory_space=pl.ANY)],
        out_specs=(vmem, vmem),
        scratch_shapes=[
            pltpu.VMEM((width, relations.shape[0]), f32),
            pltpu.VMEM((blocks, width, LANES), f32),
            pltpu.VMEM((groups, width, rows // parts), bf16),
            pltpu.VMEM((groups, width, rows // parts), bf16),
            pltpu.VMEM((width, rows), bf16),
            pltpu.VMEM((tiles, width, LANES), f32),
            pltpu.VMEM((rows, edges), bf16),
            pltpu.VMEM((rows + hubs, edges), bf16),
            pltpu.VMEM((width, edges), bf16),
            pltpu.VMEM((width, edges), bf16),
            pltpu.VMEM((tiles, edge, width), bf16),
            pltpu.VMEM((width, edges), bf16),
            pltpu.VMEM((width, edges), bf16),
            pltpu.VMEM((groups, width, rows // parts), bf16),
            pltpu.VMEM((groups, width, rows // parts), bf16),
            pltpu.VMEM((width, rows), f32),
            pltpu.VMEM((edge, edge), f32),
            pltpu.VMEM((edge, edge), f32),
            pltpu.VMEM((edge, edge), bf16),
            pltpu.VMEM((edge, edge), bf16),
            pltpu.VMEM((chunks, CHUNK_ROWS, hubs), f32),
            pltpu.VMEM((chunks, CHUNK_ROWS, hubs), bf16),
            pltpu.VMEM((members, CHUNK_ROWS, hubs), bf16),
            pltpu.VMEM((groups, CHUNK_ROWS, hubs), f32),
            pltpu.VMEM((chunks, CHUNK_ROWS, hubs), bf16),
            dma,
            dma((parts, groups)),
            dma((parts, groups)),
            dma((parts, groups)),
            dma((parts, groups)),
            dma((members,)),
            dma((members,)),
            dma((groups,)),
            dma((groups,)),
            dma((members,)),
            dma((members,)),
        ],
        compiler_params=pltpu.CompilerParams(
            collective_id=0, has_side_effects=True, vmem_limit_bytes=58 * 1024 * 1024
        ),
        cost_estimate=pl.CostEstimate(
            flops=4 * edges * width * (2 * rows + hubs + edge),
            bytes_accessed=relations.size * 4,
            transcendentals=edges * edge),
    )(tile_count, tile_rel, matching, entities.T, hub_rows.T, head_index, tail_index, relations.T)
    new_ent, new_hub = pl.pallas_call(
        hand_over,
        out_shape=(
            jax.ShapeDtypeStruct(new_ent.shape, bf16),
            jax.ShapeDtypeStruct(new_hub.shape, bf16),
        ),
        in_specs=[vmem, vmem],
        out_specs=(vmem, vmem),
    )(new_ent, new_hub)
    return new_ent.T, new_hub.T


def solution(mesh):
    placed = (
        P(("group", "member"), None),
        P(),
        P(),
        P(),
        P(("group", "member"), None),
        P(("group", "member"), None),
        P(("group", "member")),
        P("group", "member"),
    )
    return jax.shard_map(
        functools.partial(shards, mesh.shape["group"], mesh.shape["member"]),
        mesh=mesh,
        in_specs=placed,
        out_specs=(P(("group", "member"), None), P()),
        check_vma=False,
    )
```

```python
import functools

import jax
import jax.numpy as jnp
from jax import lax
from jax.experimental import pallas as pl
from jax.experimental.pallas import tpu as pltpu
from jax.sharding import PartitionSpec as P

learn_rate = 0.1
MESH = pl.DeviceIdType.MESH
LANES = 128
CHUNK_ROWS = 32
UNROLL = 4
contract_last = (((1,), (1,)), ((), ()))
f32 = jnp.float32
bf16 = jnp.bfloat16


def dot(a, b):
    return jnp.dot(a, b, preferred_element_type=f32)


def dot_last(a, b):
    return lax.dot_general(a, b, contract_last, preferred_element_type=f32)


def kernel(
    groups, members, exchange, count_ref, rel_ref, match_ref,
    ent_ref, hub_ref, head_ref, tail_ref, table_ref,
    new_ent_ref, new_hub_ref,
    landed, relations, peers_0, peers_1, table, weights, hot_head, hot_tail, picked,
    query_t, query, d_head, d_tail, back_0, back_1, head_sum,
    scores_0, scores_1, diff_0, diff_1,
    hub_pad, hub_send, hub_in, hub_mid, hub_out,
    rel_sem, ent_send, ent_recv, back_send, back_recv,
    s1, r1, s2, r2, s3, r3,
):
    g = lax.axis_index("group")
    m = lax.axis_index("member")
    width, rows = ent_ref.shape
    half = width // 2
    hubs = hub_ref.shape[1]
    tiles, edge = head_ref.shape
    rels = table_ref.shape[1]
    peers, back = (peers_0, peers_1), (back_0, back_1)
    scores_of, diff_of = (scores_0, scores_1), (diff_0, diff_1)
    parts = len(back)
    part_rows = rows // parts
    chunks = hub_send.shape[0]

    blocks = relations.shape[0]
    load = pltpu.make_async_copy(table_ref, landed, rel_sem)
    load.start()
    other_groups = [lax.rem(g + d, groups) for d in range(1, groups)]
    row_groups = other_groups if exchange else []
    other_members = [lax.rem(m + d, members) for d in range(1, members)]
    barrier = pltpu.get_barrier_semaphore()
    for o in other_groups:
        pl.semaphore_signal(barrier, inc=1, device_id=(o, m), device_id_type=MESH)
    for o in other_members:
        pl.semaphore_signal(barrier, inc=1, device_id=(g, o), device_id_type=MESH)
    pl.semaphore_wait(barrier, groups + members - 2)

    def remote(src, dst, send, recv, where):
        return pltpu.make_async_remote_copy(
            src_ref=src, dst_ref=dst, send_sem=send, recv_sem=recv,
            device_id=where, device_id_type=MESH,
        )

    def lanes_of(part):
        return pl.ds(part * part_rows, part_rows)

    def ent_copy(part, o, slot):
        return remote(ent_ref.at[:, lanes_of(part)], peers[part].at[slot],
                      ent_send.at[part, o], ent_recv.at[part, slot], (o, m))

    for part in range(parts):
        for o in row_groups:
            ent_copy(part, o, g).start()

    if exchange:
        for part in range(parts):
            peers[part][g] = ent_ref[:, lanes_of(part)]
    hub_now = hub_ref[...].astype(f32)
    for c in range(chunks):
        piece = hub_now[c * CHUNK_ROWS : (c + 1) * CHUNK_ROWS]
        hub_pad[c, : piece.shape[0], :] = piece
        if piece.shape[0] < CHUNK_ROWS:
            hub_pad[c, piece.shape[0] :, :] = jnp.zeros(
                (CHUNK_ROWS - piece.shape[0], hubs), f32)
    load.wait()
    for i in range(blocks):
        piece = landed[:, i * LANES : (i + 1) * LANES]
        if piece.shape[1] < LANES:
            piece = jnp.concatenate(
                [piece, jnp.zeros((width, LANES - piece.shape[1]), f32)], axis=1)
        relations[i] = piece
    live = count_ref[0, 0]
    lane = lax.broadcasted_iota(jnp.int32, (width, LANES), 1)

    def lanes_at(t):
        return pl.ds(pl.multiple_of(t * edge, edge), edge)

    def wide_at(t):
        return pl.ds(pl.multiple_of(t * edge, UNROLL * edge), UNROLL * edge)

    def hot(ids, n):
        return (lax.broadcasted_iota(jnp.int32, (n, edge), 0) == ids).astype(f32).astype(bf16)

    def weight_of(t):
        rel = rel_ref[t]
        block = jnp.int32(0)
        for i in range(1, blocks):
            block = jnp.where(rel >= i * LANES, i, block)
        kept = jnp.where(lane == rel - block * LANES, relations[block], 0.0)
        column = jnp.sum(kept, axis=1, keepdims=True)
        column = jnp.where(t < live, column, jnp.zeros_like(column))
        weights[t] = jnp.broadcast_to(column, (width, LANES))

    def halves(t):
        w = jnp.concatenate([weights[t]] * (edge // LANES), axis=1)
        return w[:half], w[half:]

    def prepare(first):
        group = [first + k for k in range(UNROLL)]
        for t in group:
            hot_head[:, lanes_at(t)] = hot(head_ref[pl.ds(t, 1), :], rows)
        found = [dot(ent_ref[...], hot_head[:, lanes_at(t)]) for t in group]
        for t in group:
            hot_tail[:, lanes_at(t)] = hot(tail_ref[pl.ds(t, 1), :], rows + hubs)
        queries = []
        for t, head in zip(group, found):
            wr, wi = halves(t)
            hr, hi = head[:half], head[half:]
            q = jnp.concatenate([hr * wr - hi * wi, hr * wi + hi * wr], axis=0)
            query_t[:, lanes_at(t)] = q.astype(bf16)
            queries.append(q)
        for t, q in zip(group, queries):
            query[t] = q.T.astype(bf16)
        at = wide_at(first)
        picked[:, at] = dot(hub_ref[...], hot_tail[rows:, at]).astype(bf16)

    def quads(step):
        def body(i, _):
            step(UNROLL * i)
            return 0

        lax.fori_loop(0, tiles // UNROLL, body, 0)

    for t in range(tiles):
        weight_of(t)
    quads(prepare)

    def wait_rows(part):
        if not exchange:
            table[:, lanes_of(part)] = ent_ref[:, lanes_of(part)]
            return
        for o in row_groups:
            ent_copy(part, o, o).wait_recv()
        table[:, lanes_of(part)] = peers[part][match_ref[g]]

    for part in range(parts):
        wait_rows(part)

        def add_part(first, part=part):
            at = wide_at(first)
            found = dot(table[:, lanes_of(part)], hot_tail[lanes_of(part), at])
            picked[:, at] = (found + picked[:, at].astype(f32)).astype(bf16)

        quads(add_part)

    def make_scores(t, par):
        scores_of[par][...] = dot(query[t], picked[:, lanes_at(t)])

    def make_diff(par):
        scores = scores_of[par][...]
        expo = jnp.exp(scores - jnp.max(scores, axis=1, keepdims=True))
        probs = expo * (1.0 / jnp.sum(expo, axis=1, keepdims=True))
        eye = lax.broadcasted_iota(jnp.int32, (edge, edge), 0) == lax.broadcasted_iota(
            jnp.int32, (edge, edge), 1)
        diff_of[par][...] = jnp.where(eye, probs - 1.0, probs).astype(bf16)

    def make_grads(t, par):
        at = lanes_at(t)
        diff = diff_of[par][...]
        d_tail[:, at] = dot(query_t[:, at], diff).astype(bf16)
        dq = dot_last(picked[:, at], diff)
        wr, wi = halves(t)
        dr, di = dq[:half], dq[half:]
        d_head[:, at] = jnp.concatenate(
            [dr * wr + di * wi, di * wr - dr * wi], axis=0).astype(bf16)

    def two_steps(i, _):
        for par in range(2):
            t = 2 * i + par
            make_scores(t, par)
            make_diff(1 - par)
            make_grads(t - 2, par)
        return 0

    make_scores(0, 0)
    make_scores(1, 1)
    make_diff(0)
    lax.fori_loop(1, tiles // 2, two_steps, 0)
    make_diff(1)
    make_grads(tiles - 2, 0)
    make_grads(tiles - 1, 1)

    def back_copy(part, o, slot):
        return remote(back[part].at[slot], back[part].at[slot],
                      back_send.at[part, o], back_recv.at[part, slot], (o, m))

    def send_back(part, acc):
        back[part][g] = acc.astype(bf16)
        for o in row_groups:
            back_copy(part, o, g).start()

    last = parts - 1
    acc = dot_last(d_tail[...], hot_tail[last * part_rows :, :])
    send_back(last, acc[:, :part_rows])
    for c in range(chunks):
        piece = acc[c * CHUNK_ROWS : (c + 1) * CHUNK_ROWS, part_rows:]
        if piece.shape[0] < CHUNK_ROWS:
            piece = jnp.concatenate(
                [piece, jnp.zeros((CHUNK_ROWS - piece.shape[0], hubs), f32)], axis=0)
        hub_send[c] = piece.astype(bf16)

    owner = m < chunks

    for o in other_members:
        @pl.when(o < chunks)
        def _(o=o):
            remote(hub_send.at[o], hub_in.at[m], s1.at[o], r1.at[m], (g, o)).start()

    @pl.when(owner)
    def _():
        hub_in[m] = hub_send[m]

    for part in range(last):
        send_back(part, dot_last(d_tail[...], hot_tail[lanes_of(part), :]))

    def stage_two(o, slot):
        return remote(hub_mid.at[slot], hub_mid.at[slot], s2.at[o], r2.at[slot], (o, m))

    @pl.when(owner)
    def _():
        for o in other_members:
            remote(hub_send.at[m], hub_in.at[o], s1.at[o], r1.at[o], (g, o)).wait_recv()
        total = hub_in[0].astype(f32)
        for i in range(1, members):
            total = total + hub_in[i].astype(f32)
        hub_mid[g] = total
        for o in other_groups:
            stage_two(o, g).start()

    head_sum[...] = dot_last(d_head[...], hot_head[...])

    def stage_three(o, slot):
        return remote(hub_out.at[slot], hub_out.at[slot], s3.at[o], r3.at[slot], (g, o))

    @pl.when(owner)
    def _():
        for o in other_groups:
            stage_two(o, o).wait_recv()
        total = hub_mid[0]
        for i in range(1, groups):
            total = total + hub_mid[i]
        hub_out[m] = (hub_pad[m] - learn_rate * total).astype(bf16)
        for o in other_members:
            stage_three(o, m).start()

    source = g
    if exchange:
        source = jnp.int32(0)
        for i in range(1, groups):
            source = jnp.where(match_ref[i] == g, i, source)
    for part in [last, *range(last)]:
        for o in row_groups:
            back_copy(part, o, o).wait_recv()
        at = lanes_of(part)
        grads = head_sum[:, at] + back[part][source].astype(f32)
        new_ent_ref[:, at] = (ent_ref[:, at].astype(f32) - learn_rate * grads).astype(bf16)

    for o in other_members:
        @pl.when(o < chunks)
        def _(o=o):
            stage_three(o, o).wait_recv()
    new_hub_ref[...] = hub_out[...].reshape(chunks * CHUNK_ROWS, hubs)[:width]

    for part in range(parts):
        for o in row_groups:
            ent_copy(part, o, g).wait_send()
            back_copy(part, o, g).wait_send()
    for o in other_members:
        @pl.when(o < chunks)
        def _(o=o):
            remote(hub_send.at[o], hub_in.at[m], s1.at[o], r1.at[m], (g, o)).wait_send()

    @pl.when(owner)
    def _():
        for o in other_groups:
            stage_two(o, g).wait_send()
        for o in other_members:
            stage_three(o, m).wait_send()


def hand_over(ent_ref, hub_ref, new_ent_ref, new_hub_ref):
    new_ent_ref[...] = ent_ref[...]
    new_hub_ref[...] = hub_ref[...]


def shards(groups, members, entities, hub_rows, relations, matching, head_index, tail_index, tile_rel, tile_count):
    rows, width = entities.shape
    hubs = hub_rows.shape[0]
    tiles, edge = head_index.shape
    edges = tiles * edge
    chunks = -(-width // CHUNK_ROWS)
    blocks = -(-relations.shape[0] // LANES)
    parts = 2
    smem = pl.BlockSpec(memory_space=pltpu.SMEM)
    vmem = pl.BlockSpec(memory_space=pltpu.VMEM)
    dma = pltpu.SemaphoreType.DMA
    step = lambda exchange: pl.pallas_call(
        functools.partial(kernel, groups, members, exchange),
        out_shape=(
            jax.ShapeDtypeStruct((width, rows), bf16),
            jax.ShapeDtypeStruct((width, hubs), bf16),
        ),
        in_specs=[smem, smem, smem, vmem, vmem, vmem, vmem, pl.BlockSpec(memory_space=pl.ANY)],
        out_specs=(vmem, vmem),
        scratch_shapes=[
            pltpu.VMEM((width, relations.shape[0]), f32),
            pltpu.VMEM((blocks, width, LANES), f32),
            pltpu.VMEM((groups, width, rows // parts), bf16),
            pltpu.VMEM((groups, width, rows // parts), bf16),
            pltpu.VMEM((width, rows), bf16),
            pltpu.VMEM((tiles, width, LANES), f32),
            pltpu.VMEM((rows, edges), bf16),
            pltpu.VMEM((rows + hubs, edges), bf16),
            pltpu.VMEM((width, edges), bf16),
            pltpu.VMEM((width, edges), bf16),
            pltpu.VMEM((tiles, edge, width), bf16),
            pltpu.VMEM((width, edges), bf16),
            pltpu.VMEM((width, edges), bf16),
            pltpu.VMEM((groups, width, rows // parts), bf16),
            pltpu.VMEM((groups, width, rows // parts), bf16),
            pltpu.VMEM((width, rows), f32),
            pltpu.VMEM((edge, edge), f32),
            pltpu.VMEM((edge, edge), f32),
            pltpu.VMEM((edge, edge), bf16),
            pltpu.VMEM((edge, edge), bf16),
            pltpu.VMEM((chunks, CHUNK_ROWS, hubs), f32),
            pltpu.VMEM((chunks, CHUNK_ROWS, hubs), bf16),
            pltpu.VMEM((members, CHUNK_ROWS, hubs), bf16),
            pltpu.VMEM((groups, CHUNK_ROWS, hubs), f32),
            pltpu.VMEM((chunks, CHUNK_ROWS, hubs), bf16),
            dma,
            dma((parts, groups)),
            dma((parts, groups)),
            dma((parts, groups)),
            dma((parts, groups)),
            dma((members,)),
            dma((members,)),
            dma((groups,)),
            dma((groups,)),
            dma((members,)),
            dma((members,)),
        ],
        compiler_params=pltpu.CompilerParams(
            collective_id=int(exchange), has_side_effects=True, vmem_limit_bytes=58 * 1024 * 1024
        ),
        cost_estimate=pl.CostEstimate(
            flops=4 * edges * width * (2 * rows + hubs + edge),
            bytes_accessed=relations.size * 4,
            transcendentals=edges * edge),
    )
    at_home = jnp.all(matching == jnp.arange(groups, dtype=matching.dtype))
    new_ent, new_hub = lax.cond(
        at_home, step(False), step(True),
        tile_count, tile_rel, matching, entities.T, hub_rows.T, head_index, tail_index, relations.T)
    new_ent, new_hub = pl.pallas_call(
        hand_over,
        out_shape=(
            jax.ShapeDtypeStruct(new_ent.shape, bf16),
            jax.ShapeDtypeStruct(new_hub.shape, bf16),
        ),
        in_specs=[vmem, vmem],
        out_specs=(vmem, vmem),
    )(new_ent, new_hub)
    return new_ent.T, new_hub.T


def solution(mesh):
    placed = (
        P(("group", "member"), None),
        P(),
        P(),
        P(),
        P(("group", "member"), None),
        P(("group", "member"), None),
        P(("group", "member")),
        P("group", "member"),
    )
    return jax.shard_map(
        functools.partial(shards, mesh.shape["group"], mesh.shape["member"]),
        mesh=mesh,
        in_specs=placed,
        out_specs=(P(("group", "member"), None), P()),
        check_vma=False,
    )
```

```python
import functools

import jax
import jax.numpy as jnp
from jax import lax
from jax.experimental import pallas as pl
from jax.experimental.pallas import tpu as pltpu
from jax.sharding import PartitionSpec as P

learn_rate = 0.1
MESH = pl.DeviceIdType.MESH
LANES = 128
CHUNK_ROWS = 32
UNROLL = 4
contract_last = (((1,), (1,)), ((), ()))
f32 = jnp.float32
bf16 = jnp.bfloat16


def dot(a, b):
    return jnp.dot(a, b, preferred_element_type=f32)


def dot_last(a, b):
    return lax.dot_general(a, b, contract_last, preferred_element_type=f32)


def kernel(
    groups, members, exchange, count_ref, rel_ref, match_ref,
    ent_ref, hub_ref, head_ref, tail_ref, table_ref,
    new_ent_ref, new_hub_ref,
    landed, relations, peers_0, peers_1, table, weights, hot_head, hot_tail, picked,
    query_t, query, d_head, d_tail, back_0, back_1, head_sum,
    scores_0, scores_1, diff_0, diff_1,
    hub_pad, hub_send, hub_in, hub_mid, hub_out,
    rel_sem, ent_send, ent_recv, back_send, back_recv,
    s1, r1, s2, r2, s3, r3,
):
    g = lax.axis_index("group")
    m = lax.axis_index("member")
    width, rows = ent_ref.shape
    half = width // 2
    hubs = hub_ref.shape[1]
    tiles, edge = head_ref.shape
    rels = table_ref.shape[1]
    peers, back = (peers_0, peers_1), (back_0, back_1)
    scores_of, diff_of = (scores_0, scores_1), (diff_0, diff_1)
    parts = len(back)
    part_rows = rows // parts
    chunks = hub_send.shape[0]

    blocks = relations.shape[0]
    load = pltpu.make_async_copy(table_ref, landed, rel_sem)
    load.start()
    other_groups = [lax.rem(g + d, groups) for d in range(1, groups)]
    row_groups = other_groups if exchange else []
    other_members = [lax.rem(m + d, members) for d in range(1, members)]
    barrier = pltpu.get_barrier_semaphore()
    for o in other_groups:
        pl.semaphore_signal(barrier, inc=1, device_id=(o, m), device_id_type=MESH)
    for o in other_members:
        pl.semaphore_signal(barrier, inc=1, device_id=(g, o), device_id_type=MESH)
    pl.semaphore_wait(barrier, groups + members - 2)

    def remote(src, dst, send, recv, where):
        return pltpu.make_async_remote_copy(
            src_ref=src, dst_ref=dst, send_sem=send, recv_sem=recv,
            device_id=where, device_id_type=MESH,
        )

    def lanes_of(part):
        return pl.ds(part * part_rows, part_rows)

    def ent_copy(part, o, slot):
        return remote(ent_ref.at[:, lanes_of(part)], peers[part].at[slot],
                      ent_send.at[part, o], ent_recv.at[part, slot], (o, m))

    for part in range(parts):
        for o in row_groups:
            ent_copy(part, o, g).start()

    if exchange:
        for part in range(parts):
            peers[part][g] = ent_ref[:, lanes_of(part)]
    hub_now = hub_ref[...].astype(f32)
    for c in range(chunks):
        piece = hub_now[c * CHUNK_ROWS : (c + 1) * CHUNK_ROWS]
        hub_pad[c, : piece.shape[0], :] = piece
        if piece.shape[0] < CHUNK_ROWS:
            hub_pad[c, piece.shape[0] :, :] = jnp.zeros(
                (CHUNK_ROWS - piece.shape[0], hubs), f32)
    load.wait()
    for i in range(blocks):
        piece = landed[:, i * LANES : (i + 1) * LANES]
        if piece.shape[1] < LANES:
            piece = jnp.concatenate(
                [piece, jnp.zeros((width, LANES - piece.shape[1]), f32)], axis=1)
        relations[i] = piece
    live = count_ref[0, 0]
    lane = lax.broadcasted_iota(jnp.int32, (width, LANES), 1)

    def lanes_at(t):
        return pl.ds(pl.multiple_of(t * edge, edge), edge)

    def wide_at(t):
        return pl.ds(pl.multiple_of(t * edge, UNROLL * edge), UNROLL * edge)

    def hot(ids, n):
        return (lax.broadcasted_iota(jnp.int32, (n, edge), 0) == ids).astype(f32).astype(bf16)

    def weight_of(t):
        rel = rel_ref[t]
        block = jnp.int32(0)
        for i in range(1, blocks):
            block = jnp.where(rel >= i * LANES, i, block)
        kept = jnp.where(lane == rel - block * LANES, relations[block], 0.0)
        column = jnp.sum(kept, axis=1, keepdims=True)
        column = jnp.where(t < live, column, jnp.zeros_like(column))
        weights[t] = jnp.broadcast_to(column, (width, LANES))

    def halves(t):
        w = jnp.concatenate([weights[t]] * (edge // LANES), axis=1)
        return w[:half], w[half:]

    def make_hot(t):
        hot_head[:, lanes_at(t)] = hot(head_ref[pl.ds(t, 1), :], rows)
        hot_tail[:, lanes_at(t)] = hot(tail_ref[pl.ds(t, 1), :], rows + hubs)

    def make_query(t):
        at = lanes_at(t)
        head = dot(ent_ref[...], hot_head[:, at])
        wr, wi = halves(t)
        hr, hi = head[:half], head[half:]
        query_t[:, at] = jnp.concatenate(
            [hr * wr - hi * wi, hr * wi + hi * wr], axis=0).astype(bf16)

    def turn(t):
        query[t] = query_t[:, lanes_at(t)].T

    def prepare_two(i, _):
        for par in range(2):
            t = 2 * i + par
            turn(t - 2)
            make_query(t - 1)
            make_hot(t)
        return 0

    def hub_pick(first):
        at = wide_at(first)
        picked[:, at] = dot(hub_ref[...], hot_tail[rows:, at]).astype(bf16)

    def home_pick(first):
        at = wide_at(first)
        found = dot(ent_ref[...], hot_tail[:rows, at])
        picked[:, at] = (found + dot(hub_ref[...], hot_tail[rows:, at])).astype(bf16)

    def quads(step):
        def body(i, _):
            step(UNROLL * i)
            return 0

        lax.fori_loop(0, tiles // UNROLL, body, 0)

    for t in range(tiles):
        weight_of(t)
    make_hot(0)
    make_query(0)
    make_hot(1)
    lax.fori_loop(1, tiles // 2, prepare_two, 0)
    turn(tiles - 2)
    make_query(tiles - 1)
    turn(tiles - 1)
    quads(hub_pick if exchange else home_pick)

    def wait_rows(part):
        for o in row_groups:
            ent_copy(part, o, o).wait_recv()
        table[:, lanes_of(part)] = peers[part][match_ref[g]]

    for part in range(parts if exchange else 0):
        wait_rows(part)

        def add_part(first, part=part):
            at = wide_at(first)
            found = dot(table[:, lanes_of(part)], hot_tail[lanes_of(part), at])
            picked[:, at] = (found + picked[:, at].astype(f32)).astype(bf16)

        quads(add_part)

    def make_scores(t, par):
        scores_of[par][...] = dot(query[t], picked[:, lanes_at(t)])

    def make_diff(par):
        scores = scores_of[par][...]
        expo = jnp.exp(scores - jnp.max(scores, axis=1, keepdims=True))
        probs = expo * (1.0 / jnp.sum(expo, axis=1, keepdims=True))
        eye = lax.broadcasted_iota(jnp.int32, (edge, edge), 0) == lax.broadcasted_iota(
            jnp.int32, (edge, edge), 1)
        diff_of[par][...] = jnp.where(eye, probs - 1.0, probs).astype(bf16)

    def make_grads(t, par):
        at = lanes_at(t)
        diff = diff_of[par][...]
        d_tail[:, at] = dot(query_t[:, at], diff).astype(bf16)
        dq = dot_last(picked[:, at], diff)
        wr, wi = halves(t)
        dr, di = dq[:half], dq[half:]
        d_head[:, at] = jnp.concatenate(
            [dr * wr + di * wi, di * wr - dr * wi], axis=0).astype(bf16)

    def two_steps(i, _):
        for par in range(2):
            t = 2 * i + par
            make_scores(t, par)
            make_diff(1 - par)
            make_grads(t - 2, par)
        return 0

    make_scores(0, 0)
    make_scores(1, 1)
    make_diff(0)
    lax.fori_loop(1, tiles // 2, two_steps, 0)
    make_diff(1)
    make_grads(tiles - 2, 0)
    make_grads(tiles - 1, 1)

    def back_copy(part, o, slot):
        return remote(back[part].at[slot], back[part].at[slot],
                      back_send.at[part, o], back_recv.at[part, slot], (o, m))

    def send_back(part, acc):
        back[part][g] = acc.astype(bf16)
        for o in row_groups:
            back_copy(part, o, g).start()

    last = parts - 1
    acc = dot_last(d_tail[...], hot_tail[last * part_rows :, :])
    send_back(last, acc[:, :part_rows])
    for c in range(chunks):
        piece = acc[c * CHUNK_ROWS : (c + 1) * CHUNK_ROWS, part_rows:]
        if piece.shape[0] < CHUNK_ROWS:
            piece = jnp.concatenate(
                [piece, jnp.zeros((CHUNK_ROWS - piece.shape[0], hubs), f32)], axis=0)
        hub_send[c] = piece.astype(bf16)

    owner = m < chunks

    for o in other_members:
        @pl.when(o < chunks)
        def _(o=o):
            remote(hub_send.at[o], hub_in.at[m], s1.at[o], r1.at[m], (g, o)).start()

    @pl.when(owner)
    def _():
        hub_in[m] = hub_send[m]

    for part in range(last):
        send_back(part, dot_last(d_tail[...], hot_tail[lanes_of(part), :]))

    def stage_two(o, slot):
        return remote(hub_mid.at[slot], hub_mid.at[slot], s2.at[o], r2.at[slot], (o, m))

    @pl.when(owner)
    def _():
        for o in other_members:
            remote(hub_send.at[m], hub_in.at[o], s1.at[o], r1.at[o], (g, o)).wait_recv()
        total = hub_in[0].astype(f32)
        for i in range(1, members):
            total = total + hub_in[i].astype(f32)
        hub_mid[g] = total
        for o in other_groups:
            stage_two(o, g).start()

    head_sum[...] = dot_last(d_head[...], hot_head[...])

    def stage_three(o, slot):
        return remote(hub_out.at[slot], hub_out.at[slot], s3.at[o], r3.at[slot], (g, o))

    @pl.when(owner)
    def _():
        for o in other_groups:
            stage_two(o, o).wait_recv()
        total = hub_mid[0]
        for i in range(1, groups):
            total = total + hub_mid[i]
        hub_out[m] = (hub_pad[m] - learn_rate * total).astype(bf16)
        for o in other_members:
            stage_three(o, m).start()

    source = g
    if exchange:
        source = jnp.int32(0)
        for i in range(1, groups):
            source = jnp.where(match_ref[i] == g, i, source)
    for part in [last, *range(last)]:
        for o in row_groups:
            back_copy(part, o, o).wait_recv()
        at = lanes_of(part)
        grads = head_sum[:, at] + back[part][source].astype(f32)
        new_ent_ref[:, at] = (ent_ref[:, at].astype(f32) - learn_rate * grads).astype(bf16)

    for o in other_members:
        @pl.when(o < chunks)
        def _(o=o):
            stage_three(o, o).wait_recv()
    new_hub_ref[...] = hub_out[...].reshape(chunks * CHUNK_ROWS, hubs)[:width]

    for part in range(parts):
        for o in row_groups:
            ent_copy(part, o, g).wait_send()
            back_copy(part, o, g).wait_send()
    for o in other_members:
        @pl.when(o < chunks)
        def _(o=o):
            remote(hub_send.at[o], hub_in.at[m], s1.at[o], r1.at[m], (g, o)).wait_send()

    @pl.when(owner)
    def _():
        for o in other_groups:
            stage_two(o, g).wait_send()
        for o in other_members:
            stage_three(o, m).wait_send()


def hand_over(ent_ref, hub_ref, new_ent_ref, new_hub_ref):
    new_ent_ref[...] = ent_ref[...]
    new_hub_ref[...] = hub_ref[...]


def shards(groups, members, entities, hub_rows, relations, matching, head_index, tail_index, tile_rel, tile_count):
    rows, width = entities.shape
    hubs = hub_rows.shape[0]
    tiles, edge = head_index.shape
    edges = tiles * edge
    chunks = -(-width // CHUNK_ROWS)
    blocks = -(-relations.shape[0] // LANES)
    parts = 2
    smem = pl.BlockSpec(memory_space=pltpu.SMEM)
    vmem = pl.BlockSpec(memory_space=pltpu.VMEM)
    dma = pltpu.SemaphoreType.DMA
    step = lambda exchange: pl.pallas_call(
        functools.partial(kernel, groups, members, exchange),
        out_shape=(
            jax.ShapeDtypeStruct((width, rows), bf16),
            jax.ShapeDtypeStruct((width, hubs), bf16),
        ),
        in_specs=[smem, smem, smem, vmem, vmem, vmem, vmem, pl.BlockSpec(memory_space=pl.ANY)],
        out_specs=(vmem, vmem),
        scratch_shapes=[
            pltpu.VMEM((width, relations.shape[0]), f32),
            pltpu.VMEM((blocks, width, LANES), f32),
            pltpu.VMEM((groups, width, rows // parts), bf16),
            pltpu.VMEM((groups, width, rows // parts), bf16),
            pltpu.VMEM((width, rows), bf16),
            pltpu.VMEM((tiles, width, LANES), f32),
            pltpu.VMEM((rows, edges), bf16),
            pltpu.VMEM((rows + hubs, edges), bf16),
            pltpu.VMEM((width, edges), bf16),
            pltpu.VMEM((width, edges), bf16),
            pltpu.VMEM((tiles, edge, width), bf16),
            pltpu.VMEM((width, edges), bf16),
            pltpu.VMEM((width, edges), bf16),
            pltpu.VMEM((groups, width, rows // parts), bf16),
            pltpu.VMEM((groups, width, rows // parts), bf16),
            pltpu.VMEM((width, rows), f32),
            pltpu.VMEM((edge, edge), f32),
            pltpu.VMEM((edge, edge), f32),
            pltpu.VMEM((edge, edge), bf16),
            pltpu.VMEM((edge, edge), bf16),
            pltpu.VMEM((chunks, CHUNK_ROWS, hubs), f32),
            pltpu.VMEM((chunks, CHUNK_ROWS, hubs), bf16),
            pltpu.VMEM((members, CHUNK_ROWS, hubs), bf16),
            pltpu.VMEM((groups, CHUNK_ROWS, hubs), f32),
            pltpu.VMEM((chunks, CHUNK_ROWS, hubs), bf16),
            dma,
            dma((parts, groups)),
            dma((parts, groups)),
            dma((parts, groups)),
            dma((parts, groups)),
            dma((members,)),
            dma((members,)),
            dma((groups,)),
            dma((groups,)),
            dma((members,)),
            dma((members,)),
        ],
        compiler_params=pltpu.CompilerParams(
            collective_id=int(exchange), has_side_effects=True, vmem_limit_bytes=58 * 1024 * 1024
        ),
        cost_estimate=pl.CostEstimate(
            flops=4 * edges * width * (2 * rows + hubs + edge),
            bytes_accessed=relations.size * 4,
            transcendentals=edges * edge),
    )
    at_home = jnp.all(matching == jnp.arange(groups, dtype=matching.dtype))
    new_ent, new_hub = lax.cond(
        at_home, step(False), step(True),
        tile_count, tile_rel, matching, entities.T, hub_rows.T, head_index, tail_index, relations.T)
    new_ent, new_hub = pl.pallas_call(
        hand_over,
        out_shape=(
            jax.ShapeDtypeStruct(new_ent.shape, bf16),
            jax.ShapeDtypeStruct(new_hub.shape, bf16),
        ),
        in_specs=[vmem, vmem],
        out_specs=(vmem, vmem),
    )(new_ent, new_hub)
    return new_ent.T, new_hub.T


def solution(mesh):
    placed = (
        P(("group", "member"), None),
        P(),
        P(),
        P(),
        P(("group", "member"), None),
        P(("group", "member"), None),
        P(("group", "member")),
        P("group", "member"),
    )
    return jax.shard_map(
        functools.partial(shards, mesh.shape["group"], mesh.shape["member"]),
        mesh=mesh,
        in_specs=placed,
        out_specs=(P(("group", "member"), None), P()),
        check_vma=False,
    )
```
